32 devices in a mesh: pts: 32 (over z, y, x, core).
Axes of the slice: x: 2, y: 2, z: 4, core: 2. Of those that a mesh axis runs over, the one named last changes fastest.
Arguments:
- points: bfloat16 [16384, 1024], P('pts')
- weights: bfloat16 [16384, 512], P('pts'), may hold values from -2 to 2
- node_proj: bfloat16 [512, 16384], P(None, 'pts'), may hold values from -0.125 to 0.125
- skel_idx: int32 [32, 128], P('pts'), may hold values from 0 to 511, as said below
- near_list: int32 [32, 4], P('pts'), may hold values from 0 to 31, as said below
- near_count: int32 [32], P('pts'), may hold values from 1 to 4, as said below
- far_list: int32 [32, 4], P('pts'), may hold values from 0 to 7, as said below
- far_count: int32 [32], P('pts'), may hold values from 1 to 4
Outputs:
- potential: float32 [16384, 512], P('pts')
The draws below stay inside these ranges and needn't reach their ends.
Inputs may be any that keep to these rules, and one draw needn't show every extreme that they name: `skel_idx`: each row holds 128 distinct local point indices. `near_list`: row t lists distinct leaves among t - 2, t - 1, t + 1, t + 2 in its first near_count[t] slots; the other slots hold t. `near_count`: at most the number of leaves among t - 2 to t + 2 other than t. `far_list`: row t lists distinct nodes that hold none of the leaves t - 2 to t + 2 in its first far_count[t] slots; the other slots repeat the first entry.
All inputs are finite; a program needn't handle non-finite values.
Results may differ from the reference program's by a relative error of at most 0.003.
Values may be sent and summed in bfloat16 or wider, within the bound.
No kernel may reach another device: no remote copies, remote signals or barrier semaphores. Data moves between devices by JAX's collectives and lax.ppermute only.
A program may use at most 128 MiB of HBM per device.

```python
import math
import jax
import jax.numpy as jnp
from jax import lax

DIM = 1024
WCOLS = 512
SKEL = 512
NODES = 8
NEAR = 4
FAR = 4
PTS_DEV = 512
GROUP = 4
SKL = 128
TOTAL = 16384
N_PTS = 32


def coord_scale(key):
    order = jax.random.permutation(jax.random.fold_in(key, 53), DIM)
    heavy = math.sqrt(0.5 * DIM / 16.0)
    light = math.sqrt(0.5 * DIM / (DIM - 16.0))
    scale = jnp.where(order < 16, jnp.float32(heavy), jnp.float32(light))
    return scale.astype(jnp.float32)[None, :]


def draw_points(key, part):
    keys = jax.random.split(key, 3)
    group = N_PTS // NODES
    scale = coord_scale(key)
    centres = jnp.clip(jax.random.normal(keys[0], (NODES, DIM), jnp.float32), -6.0, 6.0)
    offsets = jnp.clip(jax.random.normal(keys[1], (N_PTS, DIM), jnp.float32), -6.0, 6.0)
    noise = jnp.clip(jax.random.normal(keys[2], (PTS_DEV * N_PTS, DIM), jnp.float32), -6.0, 6.0)
    node_part = jnp.repeat(centres, group * PTS_DEV, axis=0)
    leaf_part = jnp.repeat(offsets * scale, PTS_DEV, axis=0)
    total = node_part + leaf_part + 1.2247 * noise * scale
    return total.astype(jnp.bfloat16)


def draw_skel_idx(key, part):
    keys = jax.random.split(jax.random.fold_in(key, 11), N_PTS)

    def pick(single):
        return jnp.sort(jax.random.permutation(single, PTS_DEV)[:SKL])
    return jax.vmap(pick)(keys).astype(jnp.int32)


def near_helper(key):
    base = jax.random.fold_in(key, 23)
    first, second = jax.random.split(base)
    leaf = jnp.arange(N_PTS, dtype=jnp.int32)[:, None]
    offsets = jnp.array([[-2, -1, 1, 2]], dtype=jnp.int32)
    cand = leaf + offsets
    valid = ((cand >= 0) & (cand < N_PTS)).astype(jnp.int32)
    noise = jax.random.randint(first, (N_PTS, 4), 0, 1 << 20)
    order = jnp.argsort(noise + (1 - valid) * (1 << 21), axis=1, stable=True)
    cand_sorted = jnp.take_along_axis(cand, order, axis=1)
    nvalid = jnp.sum(valid, axis=1)
    draw_count = jax.random.randint(second, (N_PTS,), 0, 1 << 20) % nvalid + 1
    count = jnp.where(leaf[:, 0] == 2, nvalid, draw_count).astype(jnp.int32)
    slots = jnp.arange(4, dtype=jnp.int32)[None, :]
    listed = jnp.where(slots < count[:, None], cand_sorted, leaf).astype(jnp.int32)
    return (listed, count)


def draw_near_list(key, part):
    return near_helper(key)[0]


def draw_near_count(key, part):
    return near_helper(key)[1]


def far_helper(key):
    base = jax.random.fold_in(key, 37)
    first, second = jax.random.split(base)
    leaf = jnp.arange(N_PTS, dtype=jnp.int32)
    group = N_PTS // NODES
    nodes = jnp.arange(NODES, dtype=jnp.int32)[None, :]
    excluded = jnp.zeros((N_PTS, NODES), jnp.int32)
    for offset in range(-2, 3):
        near_node = jnp.clip(leaf + offset, 0, N_PTS - 1) // group
        excluded = jnp.maximum(excluded, (near_node[:, None] == nodes).astype(jnp.int32))
    noise = jax.random.randint(first, (N_PTS, NODES), 0, 1 << 20)
    favoured = (leaf[:, None] == 0) & (nodes == NODES - 1)
    noise = jnp.where(favoured, -1, noise)
    order = jnp.argsort(noise + excluded * (1 << 21), axis=1, stable=True)[:, :FAR].astype(jnp.int32)
    draw_count = jax.random.randint(second, (N_PTS,), 0, 1 << 20) % FAR + 1
    count = jnp.where(leaf == 0, FAR, draw_count).astype(jnp.int32)
    slots = jnp.arange(FAR, dtype=jnp.int32)[None, :]
    listed = jnp.where(slots < count[:, None], order, order[:, :1]).astype(jnp.int32)
    return (listed, count)


def draw_far_list(key, part):
    return far_helper(key)[0]


def draw_far_count(key, part):
    return far_helper(key)[1]


def level_of(rng, dims, cuts, least, high):
    factor_of, own = 1.0, jax.random.fold_in(rng, 6)
    for dim, shards_of in cuts:
        draws = jnp.exp(jax.random.uniform(jax.random.fold_in(own, dim), (shards_of,), jnp.float32, least / len(cuts), high / len(cuts)))
        factor_of = factor_of * jnp.repeat(draws, dims[dim] // shards_of).reshape([-1 if axis == dim else 1 for axis in range(len(dims))])
    return factor_of


def centred(stream_key, extent, deviation, limit, shards=(), kind=jnp.bfloat16):
    values = deviation * jax.random.normal(stream_key, extent, jnp.float32)
    if shards:
        values = values * level_of(stream_key, extent, shards, -0.22, 0.18)
    return jnp.clip(values, -limit, limit).astype(kind)


def setup_inputs(seed: int = 0) -> dict:
    arg_keys = jax.random.split(jax.random.key(seed), 9)
    return {
        "points": draw_points(jax.random.fold_in(arg_keys[8], 71), 0),
        "weights": centred(arg_keys[1], (TOTAL, WCOLS), 0.15, 2.0, ((0, 32),)),
        "node_proj": centred(arg_keys[2], (SKEL, TOTAL), (PTS_DEV * GROUP) ** -0.5, 0.125, ((1, 32),)),
        "skel_idx": draw_skel_idx(jax.random.fold_in(arg_keys[8], 71), 0),
        "near_list": draw_near_list(jax.random.fold_in(arg_keys[8], 71), 0),
        "near_count": draw_near_count(jax.random.fold_in(arg_keys[8], 71), 0),
        "far_list": draw_far_list(jax.random.fold_in(arg_keys[8], 71), 0),
        "far_count": draw_far_count(jax.random.fold_in(arg_keys[8], 71), 0),
    }


def kernel_sum(xpts, xsq, ypts, ysq, wts, gate):
    scores = lax.dot_general(xpts, ypts, (((1,), (1,)), ((), ())), preferred_element_type=jnp.float32)
    dist = xsq[:, None] + ysq[None, :] - 2.0 * scores
    kern = (jnp.exp(dist * (-0.5 / DIM)) * gate).astype(jnp.bfloat16)
    return jnp.dot(kern, wts, preferred_element_type=jnp.float32)


def reference(points, weights, node_proj, skel_idx, near_list, near_count, far_list, far_count):
    sq = jnp.sum(jnp.square(points.astype(jnp.float32)), axis=1)
    leaf_pts = points.reshape(N_PTS, PTS_DEV, DIM)
    leaf_sq = sq.reshape(N_PTS, PTS_DEV)
    leaf_w = weights.reshape(N_PTS, PTS_DEV, WCOLS)
    index = skel_idx.astype(jnp.int32)
    skel_pts = jnp.take_along_axis(leaf_pts, index[:, :, None], axis=1).reshape(NODES, SKEL, DIM)
    skel_sq = jnp.take_along_axis(leaf_sq, index, axis=1).reshape(NODES, SKEL)
    proj_leaf = jnp.transpose(node_proj.reshape(SKEL, N_PTS, PTS_DEV), (1, 0, 2))

    def partial_of(pair):
        return jnp.dot(pair[0], pair[1], preferred_element_type=jnp.float32)

    partials = lax.map(partial_of, (proj_leaf, leaf_w))
    group = N_PTS // NODES
    skel_w = jnp.sum(partials.reshape(NODES, group, SKEL, WCOLS), axis=1).astype(jnp.bfloat16)

    def one_leaf(target):
        xpts = leaf_pts[target]
        xsq = leaf_sq[target]
        total = kernel_sum(xpts, xsq, xpts, xsq, leaf_w[target], jnp.float32(1.0))
        for slot in range(NEAR):
            source = near_list[target, slot]
            gate = (slot < near_count[target]).astype(jnp.float32)
            total = total + kernel_sum(xpts, xsq, leaf_pts[source], leaf_sq[source], leaf_w[source], gate)
        for slot in range(FAR):
            node = far_list[target, slot]
            gate = (slot < far_count[target]).astype(jnp.float32)
            total = total + kernel_sum(xpts, xsq, skel_pts[node], skel_sq[node], skel_w[node], gate)
        return total

    result = lax.map(one_leaf, jnp.arange(N_PTS, dtype=jnp.int32))
    return result.reshape(N_PTS * PTS_DEV, WCOLS)
```

```python
import functools

import jax
import jax.numpy as jnp
from jax import lax
from jax.experimental import pallas as pl
from jax.experimental.pallas import tpu as pltpu
from jax.sharding import PartitionSpec as P

NODES = 8
NEAR = 4
FAR = 4
QUAD = 4
F32 = jnp.float32
BF16 = jnp.bfloat16
MIB = 1 << 20

NEAR_COUNT = NEAR
FAR_LIST = NEAR + 1
FAR_COUNT = FAR_LIST + FAR
LEAF = FAR_COUNT + 1
META = 16


def vmem():
    return pl.BlockSpec(memory_space=pltpu.VMEM)


def smem():
    return pl.BlockSpec(memory_space=pltpu.SMEM)


def params():
    return pltpu.CompilerParams(vmem_limit_bytes=48 * MIB)


def norm_column(points):
    wide = points.astype(F32)
    return jnp.sum(wide * wide, axis=1, keepdims=True)


def norm_row(points):
    column = norm_column(points)
    return jnp.transpose(jnp.broadcast_to(column, (column.shape[0], 128)))[0:1, :]


def listed(meta, row, first, count, value):
    hit = jnp.bool_(False)
    for slot in range(count):
        hit = hit | ((meta[row, first + slot] == value) & (slot < meta[row, first + count]))
    return hit


def near_hit(meta, row, leaf):
    return listed(meta, row, 0, NEAR, leaf)


def far_hit(meta, row, node):
    return listed(meta, row, FAR_LIST, FAR, node)


def add_terms(acc, xpts, xsq, ypts, ysq, wts, gate):
    rows = xpts.shape[0]
    step = min(256, rows)
    dim = xpts.shape[1]
    for first in range(0, rows, step):
        part = pl.ds(first, step)
        scores = lax.dot_general(
            xpts[part, :], ypts, (((1,), (1,)), ((), ())), preferred_element_type=F32
        )
        dist = xsq[first : first + step] + ysq - 2.0 * scores
        kern = jnp.exp(dist * (-0.5 / dim))
        if gate is not None:
            kern = kern * gate
        acc[part, :] += jnp.dot(kern.astype(BF16), wts, preferred_element_type=F32)


def prepare_body(group, idx, pts, wts, proj, skel, keep, give, whole):
    core = lax.axis_index("pts") % 2
    rows = pts.shape[0]
    count = idx.shape[1]
    whole[...] = jnp.dot(proj[...], wts[...], preferred_element_type=F32).reshape(whole.shape)
    keep[...] = whole[:, core]
    give[...] = whole[:, 1 - core].astype(BF16)
    place = lax.broadcasted_iota(jnp.int32, (rows, count), 0)
    pick = (place == idx[...]).astype(F32).astype(BF16)
    skel[...] = lax.dot_general(
        pick, pts[...], (((0,), (0,)), ((), ())), preferred_element_type=F32
    ).astype(BF16)


def prepare(group, pts, wts, proj, idx):
    count = idx.shape[1]
    wcols = wts.shape[1]
    half = (group // 2, count, wcols)
    return pl.pallas_call(
        functools.partial(prepare_body, group),
        out_shape=(
            jax.ShapeDtypeStruct((count, pts.shape[1]), BF16),
            jax.ShapeDtypeStruct(half, F32),
            jax.ShapeDtypeStruct(half, BF16),
        ),
        in_specs=[vmem()] * 4,
        out_specs=(vmem(),) * 3,
        scratch_shapes=[pltpu.VMEM((group // 2, 2, count, wcols), F32)],
        compiler_params=params(),
        cost_estimate=pl.CostEstimate(
            flops=2 * proj.size * wcols + 2 * count * pts.size, bytes_accessed=4 * MIB, transcendentals=0
        ),
    )(idx, pts, wts, proj)


def own_body(meta, ypts, wts, *refs):
    leaf = meta[0, LEAF]
    count = len(refs) // 2
    ysq = norm_row(ypts[...])
    for place in range(count):
        xpts, acc = refs[place], refs[count + place]
        acc[...] = jnp.zeros_like(acc)
        row = meta.shape[0] - count + place if meta.shape[0] > 1 else 0

        def work(xpts=xpts, acc=acc):
            add_terms(acc, xpts, norm_column(xpts[...]), ypts[...], ysq, wts[...], None)

        if row == 0:
            work()
        else:
            pl.when(near_hit(meta, row, leaf))(work)


def pair_cost(pairs, rows, dim, wcols):
    return pl.CostEstimate(
        flops=2 * pairs * rows * rows * (dim + wcols),
        bytes_accessed=pairs * rows * (2 * dim + 4 * wcols),
        transcendentals=pairs * rows * rows,
    )


def own_terms(meta, ypts, wts, targets):
    rows, wcols = wts.shape
    return pl.pallas_call(
        own_body,
        out_shape=(jax.ShapeDtypeStruct((rows, wcols), F32),) * len(targets),
        in_specs=[smem()] + [vmem()] * (2 + len(targets)),
        out_specs=(vmem(),) * len(targets),
        compiler_params=params(),
        cost_estimate=pair_cost(len(targets), rows, ypts.shape[1], wcols),
    )(meta, ypts, wts, *targets)


def far_body(group, flip, turns, first, targets, casts, meta, *refs):
    shards = len(turns)
    skel, wts = refs[:shards], refs[shards : 2 * shards]
    xpts = refs[2 * shards : 2 * shards + targets]
    start = refs[2 * shards + targets : 2 * shards + 2 * targets]
    outs = refs[2 * shards + 2 * targets : 2 * shards + 3 * targets]
    work = refs[2 * shards + 3 * targets]
    quads = lax.axis_size("pts") // QUAD
    mine = meta[0, LEAF] // QUAD
    count = skel[0].shape[0]
    nodes = []
    for turn in turns:
        deep = (mine // 2 - turn + quads // 2) % (quads // 2)
        side = (mine + flip) % 2
        nodes.append((deep * 2 + side) * QUAD // group)
    per = max(1, min(shards, 256 // count))
    squares = [norm_row(ref[...]) for ref in skel]
    for place in range(targets):
        work[...] = start[place][...]
        xsq = norm_column(xpts[place][...])
        for low in range(0, shards, per):
            high = min(shards, low + per)
            hits = [far_hit(meta, first + place, node) for node in nodes[low:high]]
            some = functools.reduce(jnp.logical_or, hits)

            @pl.when(some)
            def _(place=place, xsq=xsq, low=low, high=high, hits=hits):
                gate = jnp.concatenate(
                    [jnp.full((1, count), hit.astype(F32), F32) for hit in hits], axis=1
                )
                ysq = jnp.concatenate(squares[low:high], axis=1)
                ypts = jnp.concatenate([ref[...] for ref in skel[low:high]], axis=0)
                values = jnp.concatenate([ref[...] for ref in wts[low:high]], axis=0)
                add_terms(work, xpts[place], xsq, ypts, ysq, values, gate)

        outs[place][...] = work[...].astype(outs[place].dtype)


def far_terms(group, flip, turns, first, meta, skel, wts, xpts, start, kinds):
    rows, wcols = start[0].shape
    targets = len(xpts)
    return pl.pallas_call(
        functools.partial(far_body, group, flip, turns, first, targets, kinds),
        out_shape=tuple(jax.ShapeDtypeStruct((rows, wcols), kind) for kind in kinds),
        in_specs=[smem()] + [vmem()] * (2 * len(skel) + 2 * targets),
        out_specs=(vmem(),) * targets,
        scratch_shapes=[pltpu.VMEM((rows, wcols), F32)],
        compiler_params=params(),
        cost_estimate=pair_cost(targets, rows, xpts[0].shape[1], wcols),
    )(meta, *skel, *wts, *xpts, *start)


def cross_body(meta, xpts, start, extra, *refs):
    leaf = meta[0, LEAF]
    outer = leaf // 2 % 2
    ways = (2 * outer - 1, 2 * (2 * outer - 1))
    acc = refs[-1]
    acc[...] = start[...] + extra[...].astype(F32)
    xsq = norm_column(xpts[...])
    for place, way in ((0, ways[1]), (1, ways[0])):
        ypts, wts = refs[2 * place], refs[2 * place + 1]
        hit = near_hit(meta, 0, leaf + way)
        if place == 1:
            hit = hit & (leaf % 2 == outer)

        @pl.when(hit)
        def _(ypts=ypts, wts=wts):
            add_terms(acc, xpts, xsq, ypts[...], norm_row(ypts[...]), wts[...], None)


def cross_terms(meta, xpts, start, extra, sources):
    return pl.pallas_call(
        cross_body,
        out_shape=jax.ShapeDtypeStruct(start.shape, F32),
        in_specs=[smem()] + [vmem()] * (3 + len(sources)),
        out_specs=vmem(),
        compiler_params=params(),
        cost_estimate=pair_cost(2, start.shape[0], xpts.shape[1], start.shape[1]),
    )(meta, xpts, start, extra, *sources)


def shards(points, weights, node_proj, skel_idx, near_list, near_count, far_list, far_count):
    leaves = lax.axis_size("pts")
    me = lax.axis_index("pts")
    group = leaves // NODES
    quads = leaves // QUAD
    depth = quads // 2

    def move(value, where):
        pairs = [(source, where(source)) for source in range(leaves)]
        return lax.ppermute(value, "pts", [(a, b) for a, b in pairs if b is not None])

    def bit(level):
        return lambda source: source ^ (1 << level)

    def deeper(turn):
        def where(source):
            quad, place = divmod(source, QUAD)
            deep, side = divmod(quad, 2)
            return ((deep + turn) % depth * 2 + side) * QUAD + place

        return where

    def across(source):
        target = source + 2 if source // 2 % 2 else source - 2
        return target if 0 <= target < leaves else None

    def inward(source):
        return source ^ 1 if source % 2 != source // 2 % 2 else None

    core, side, row = bit(0), bit(1), bit(2)

    meta = jnp.concatenate(
        [near_list[0], near_count, far_list[0], far_count, me[None], jnp.zeros((META - LEAF - 1,), jnp.int32)]
    )[None]
    meta = jnp.concatenate([meta, move(meta, core)], axis=0)
    meta = jnp.concatenate([meta, move(meta, side)], axis=0)

    skel, keep, give = prepare(group, points, weights, node_proj, skel_idx)

    level = 0
    while True:
        keep = keep + move(give, bit(level)).astype(F32)
        level += 1
        if keep.shape[0] == 1:
            break
        count = keep.shape[0]
        keep = keep.reshape(count // 2, 2, *keep.shape[1:])
        upper = (me >> level) % 2 == 1
        give = jnp.where(upper, keep[:, 0], keep[:, 1]).astype(BF16)
        keep = jnp.where(upper, keep[:, 1], keep[:, 0])
    share = keep[0].astype(BF16)

    pts_core = move(points, core)
    pts_side = move(points, side)
    pts_both = move(pts_side, core)

    skel_z = [skel] + [move(skel, deeper(turn)) for turn in range(1, depth)]
    share_z = [share] + [move(share, deeper(turn)) for turn in range(1, depth)]
    skel_y = [move(value, row) for value in skel_z]
    share_y = [move(value, row) for value in share_z]

    cross_p = move(points, across)
    cross_w = move(weights, across)
    cross_pm = move(cross_p, inward)
    cross_wm = move(cross_w, inward)

    turns = tuple(range(depth))
    acc0, acc1 = own_terms(meta[:2], points, weights, (points, pts_core))
    acc2, acc3 = own_terms(meta, points, weights, (pts_side, pts_both))
    acc0, acc1, acc2, acc3 = far_terms(
        group, 0, turns, 0, meta, skel_z, share_z,
        (points, pts_core, pts_side, pts_both), (acc0, acc1, acc2, acc3), (F32,) * 4,
    )
    acc2, out3 = far_terms(
        group, 1, turns, 2, meta, skel_y, share_y, (pts_side, pts_both), (acc2, acc3), (F32, BF16)
    )
    out2 = (acc2 + move(out3, core).astype(F32)).astype(BF16)
    last = move(out2, side)
    acc0, out1 = far_terms(
        group, 1, turns, 0, meta, skel_y, share_y, (points, pts_core), (acc0, acc1), (F32, BF16)
    )
    extra = move(out1, core)
    total = cross_terms(meta, points, acc0, extra, (cross_p, cross_w, cross_pm, cross_wm))
    return total + last.astype(F32)


def solution(mesh):
    in_specs = (
        P("pts", None),
        P("pts", None),
        P(None, "pts"),
        P("pts", None),
        P("pts", None),
        P("pts"),
        P("pts", None),
        P("pts"),
    )
    out_specs = P("pts", None)
    return jax.shard_map(shards, mesh=mesh, in_specs=in_specs, out_specs=out_specs, check_vma=False)
```

```python
import functools
import math

import jax
import jax.numpy as jnp
from jax import lax
from jax.experimental import pallas as pl
from jax.experimental.pallas import tpu as pltpu
from jax.sharding import PartitionSpec as P

NODES = 8
NEAR = 4
FAR = 4
QUAD = 4
F32 = jnp.float32
BF16 = jnp.bfloat16
MIB = 1 << 20

NEAR_COUNT = NEAR
FAR_LIST = NEAR + 1
FAR_COUNT = FAR_LIST + FAR
LEAF = FAR_COUNT + 1
META = 16


def vmem():
    return pl.BlockSpec(memory_space=pltpu.VMEM)


def smem():
    return pl.BlockSpec(memory_space=pltpu.SMEM)


def params():
    return pltpu.CompilerParams(vmem_limit_bytes=24 * MIB)


def norm_column(points, scale):
    wide = points.astype(F32)
    return jnp.sum(wide * wide, axis=1, keepdims=True) * scale


def norm_row(points, scale):
    column = norm_column(points, scale)
    return jnp.transpose(jnp.broadcast_to(column, (column.shape[0], 128)))[0:1, :]


def listed(meta, row, first, count, value):
    hit = jnp.bool_(False)
    for slot in range(count):
        hit = hit | ((meta[row, first + slot] == value) & (slot < meta[row, first + count]))
    return hit


def near_hit(meta, row, leaf):
    return listed(meta, row, 0, NEAR, leaf)


def far_hit(meta, row, node):
    return listed(meta, row, FAR_LIST, FAR, node)


def half_scale(dim):
    return 0.5 * math.log2(math.e) / dim


def kernel_sum(xpts, xsq, ypts, ysq, wts):
    dim = xpts.shape[1]
    scores = lax.dot_general(
        xpts, ypts, (((1,), (1,)), ((), ())), preferred_element_type=F32
    )
    kern = jnp.exp2(scores * (2.0 * half_scale(dim)) - xsq - ysq)
    return jnp.dot(kern.astype(BF16), wts, preferred_element_type=F32)


def call(body, kinds, scalars, arrays, scratch=()):
    return pl.pallas_call(
        body,
        out_shape=kinds,
        in_specs=[smem()] * len(scalars) + [vmem()] * len(arrays),
        out_specs=jax.tree.map(lambda _: vmem(), kinds),
        scratch_shapes=scratch,
        compiler_params=params(),
        cost_estimate=pl.CostEstimate(flops=1000, bytes_accessed=1000, transcendentals=0),
    )(*scalars, *arrays)


def project_body(wts, proj, keep, give, whole):
    core = lax.axis_index("pts") % 2
    whole[...] = jnp.dot(proj[...], wts[...], preferred_element_type=F32).reshape(whole.shape)
    keep[...] = whole[:, core]
    give[...] = whole[:, 1 - core].astype(BF16)


def project(group, wts, proj):
    count, wcols = proj.shape[0] // group, wts.shape[1]
    half = (group // 2, count, wcols)
    return call(
        project_body,
        (jax.ShapeDtypeStruct(half, F32), jax.ShapeDtypeStruct(half, BF16)),
        (),
        (wts, proj),
        [pltpu.VMEM((group // 2, 2, count, wcols), F32)],
    )


def pack_body(idx, pts, keep, got, packed):
    rows, dim = pts.shape
    place = lax.broadcasted_iota(jnp.int32, (rows, idx.shape[1]), 0)
    pick = (place == idx[...]).astype(F32).astype(BF16)
    packed[:, :dim] = lax.dot_general(
        pick, pts[...], (((0,), (0,)), ((), ())), preferred_element_type=F32
    ).astype(BF16)
    packed[:, dim:] = (keep[0] + got[0].astype(F32)).astype(BF16)


def pack(idx, pts, keep, got):
    shape = (idx.shape[1], pts.shape[1] + keep.shape[2])
    return call(pack_body, jax.ShapeDtypeStruct(shape, BF16), (), (idx, pts, keep, got))


def quad_body(group, places, first, own, meta, *refs):
    packed, refs = refs[: len(places)], refs[len(places) :]
    xpts, refs = refs[:2], refs[2:]
    if own:
        mine, mine_w, *outs = refs
    else:
        start, outs = refs[:2], refs[2:]
    dim = xpts[0].shape[1]
    scale = half_scale(dim)
    quads = lax.axis_size("pts") // QUAD
    leaf = meta[0, LEAF]
    quad = leaf // QUAD
    count = packed[0].shape[0]
    nodes = []
    for turn, flip in places:
        deep = (quad // 2 - turn + quads // 2) % (quads // 2)
        nodes.append((deep * 2 + (quad + flip) % 2) * QUAD // group)
    everything = jnp.concatenate([ref[...] for ref in packed], axis=0)
    ypts, wts = everything[:, :dim], everything[:, dim:]
    ysq = norm_row(ypts, scale)
    if own:
        own_sq = norm_row(mine[...], scale)
    for place in range(2):
        hits = [far_hit(meta, first + place, node) for node in nodes]
        some = functools.reduce(jnp.logical_or, hits)
        away = [jnp.full((1, count), jnp.where(hit, 0.0, 1e30), F32) for hit in hits]
        far_sq = ysq + jnp.concatenate(away, axis=1)
        xsq = norm_column(xpts[place][...], scale)

        def far(place=place, xsq=xsq, far_sq=far_sq):
            return kernel_sum(xpts[place][...], xsq, ypts, far_sq, wts)

        out = outs[place]
        if own:
            def near(place=place, xsq=xsq):
                return kernel_sum(xpts[place][...], xsq, mine[...], own_sq, mine_w[...])

            if first + place == 0:
                out[...] = near()
            else:
                hit = near_hit(meta, first + place, leaf)

                @pl.when(hit)
                def _(out=out, near=near):
                    out[...] = near()

                @pl.when(jnp.logical_not(hit))
                def _(out=out):
                    out[...] = jnp.zeros_like(out)

            @pl.when(some)
            def _(out=out, far=far):
                out[...] += far()
        else:
            @pl.when(some)
            def _(out=out, far=far, place=place):
                out[...] = (start[place][...] + far()).astype(out.dtype)

            @pl.when(jnp.logical_not(some))
            def _(out=out, place=place):
                out[...] = start[place][...].astype(out.dtype)


def quad_terms(group, places, first, meta, packed, xpts, mine, start, kinds):
    rows = xpts[0].shape[0]
    wcols = packed[0].shape[1] - xpts[0].shape[1]
    body = functools.partial(quad_body, group, tuple(places), first, bool(mine))
    shapes = tuple(jax.ShapeDtypeStruct((rows, wcols), kind) for kind in kinds)
    return call(body, shapes, (meta,), (*packed, *xpts, *mine, *start))


def sum_body(one, two, out):
    out[...] = (one[...] + two[...].astype(F32)).astype(BF16)


def sum_terms(one, two):
    return call(sum_body, jax.ShapeDtypeStruct(one.shape, BF16), (), (one, two))


def cross_body(meta, own, other, start, start_other, ypts, wts, acc, *halves):
    leaf = meta[0, LEAF]
    away = leaf + 4 * (leaf // 2 % 2) - 2
    scale = half_scale(own.shape[1])
    ysq = norm_row(ypts[...], scale)

    def term(xpts):
        return kernel_sum(xpts[...], norm_column(xpts[...], scale), ypts[...], ysq, wts[...])

    acc[...] = start[...]
    hit = near_hit(meta, 0, away)

    @pl.when(hit)
    def _():
        acc[...] += term(own)

    def put(value):
        first = 0
        for half in halves:
            half[...] = value[first : first + half.shape[0]].astype(BF16)
            first += half.shape[0]

    hit = near_hit(meta, 1, away)

    @pl.when(hit)
    def _():
        put(start_other[...] + term(other))

    @pl.when(jnp.logical_not(hit))
    def _():
        put(start_other[...])


def cross_terms(meta, xpts, start, ypts, wts):
    rows, wcols = start[0].shape
    half = jax.ShapeDtypeStruct((rows // 2, wcols), BF16)
    shapes = (jax.ShapeDtypeStruct((rows, wcols), F32), half, half)
    return call(cross_body, shapes, (meta,), (*xpts, *start, ypts, wts))


def shards(points, weights, node_proj, skel_idx, near_list, near_count, far_list, far_count):
    leaves = lax.axis_size("pts")
    me = lax.axis_index("pts")
    group = leaves // NODES
    quads = leaves // QUAD
    depth = quads // 2

    def move(value, where):
        pairs = [(source, where(source)) for source in range(leaves)]
        return lax.ppermute(value, "pts", [(a, b) for a, b in pairs if b is not None])

    def bit(level):
        return lambda source: source ^ (1 << level)

    def deeper(turn):
        def where(source):
            quad, place = divmod(source, QUAD)
            deep, side = divmod(quad, 2)
            return ((deep + turn) % depth * 2 + side) * QUAD + place

        return where

    def after(values):
        return lax.optimization_barrier(values)

    def across(source):
        target = source + 2 if source // 2 % 2 else source - 2
        return target if 0 <= target < leaves else None

    def along(source):
        target = source - QUAD if source // 2 % 2 else source + QUAD
        return target if 0 <= target < leaves else None

    core, side, row = bit(0), bit(1), bit(2)

    meta = jnp.concatenate(
        [near_list[0], near_count, far_list[0], far_count, me[None], jnp.zeros((META - LEAF - 1,), jnp.int32)]
    )[None]
    keep, give = project(group, weights, node_proj)
    level = 0
    while True:
        got = move(give, bit(level))
        if level < 2:
            got, lists = after((got, move(meta, bit(level))))
            meta = jnp.concatenate([meta, lists], axis=0)
        level += 1
        if keep.shape[0] == 1:
            break
        count = keep.shape[0]
        keep = (keep + got.astype(F32)).reshape(count // 2, 2, *keep.shape[1:])
        upper = (me >> level) % 2 == 1
        give = jnp.where(upper, keep[:, 0], keep[:, 1]).astype(BF16)
        keep = jnp.where(upper, keep[:, 1], keep[:, 0])
    cross_w = move(weights, across)
    got, meta, cross_w = after((got, meta, cross_w))
    packed = pack(skel_idx, points, keep, got)

    up, down = deeper(1), deeper(depth - 1)
    top = depth // 2
    gathered = {(0, 0): packed}
    packed, pts_later = after((packed, points))
    pts_side = move(pts_later, side)
    pts_core = move(pts_later, core)
    gathered[1, 0] = move(packed, up)
    gathered[0, 1] = move(packed, row)
    gathered, packed = after((gathered, packed))
    if depth > 2:
        gathered[depth - 1, 0] = move(packed, down)
    gathered[1, 1] = move(gathered[1, 0], row)
    gathered, pts_side = after((gathered, pts_side))
    pts_both = move(pts_side, core)
    first_places = sorted(set(gathered) - {(1, 1)})
    if depth > 2:
        gathered[depth - 1, 1] = move(gathered[depth - 1, 0], row)
    for turn in range(2, top + 1):
        gathered[turn, 0] = move(gathered[turn - 1, 0], up)
    for turn in range(depth - 2, top, -1):
        gathered[turn, 0] = move(gathered[turn + 1, 0], down)

    mine = (points, weights)
    near_x = (points, pts_core)
    side_x = (pts_side, pts_both)
    some = [gathered[place] for place in first_places]
    acc0, acc1 = quad_terms(group, first_places, 0, meta, some, near_x, mine, (), (F32, F32))
    acc2, acc3 = quad_terms(group, first_places, 2, meta, some, side_x, mine, (), (F32, F32))
    gathered, acc0, acc1, acc2, acc3, pts_last = after((gathered, acc0, acc1, acc2, acc3, pts_side))

    for turn in range(2, top + 1):
        gathered[turn, 1] = move(gathered[turn - 1, 1], up)
    for turn in range(depth - 2, top, -1):
        gathered[turn, 1] = move(gathered[turn + 1, 1], down)
    cross_p = move(pts_last, along)
    last_places = sorted(set(gathered) - set(first_places))
    rest = [gathered[place] for place in last_places]
    acc2, out3 = quad_terms(
        group, last_places, 2, meta, rest, side_x, (), (acc2, acc3), (F32, BF16)
    )
    got3 = move(out3, core)
    acc0, acc1 = quad_terms(group, last_places, 0, meta, rest, near_x, (), (acc0, acc1), (F32, F32))
    got3, acc0, acc1 = after((got3, acc0, acc1))
    last = move(sum_terms(acc2, got3), side)
    acc0, *out1 = cross_terms(meta, near_x, (acc0, acc1), cross_p, cross_w)
    extra = jnp.concatenate([move(half, core) for half in out1], axis=0)
    return acc0 + extra.astype(F32) + last.astype(F32)


def solution(mesh):
    in_specs = (
        P("pts", None),
        P("pts", None),
        P(None, "pts"),
        P("pts", None),
        P("pts", None),
        P("pts"),
        P("pts", None),
        P("pts"),
    )
    out_specs = P("pts", None)
    return jax.shard_map(shards, mesh=mesh, in_specs=in_specs, out_specs=out_specs, check_vma=False)
```

```python
import functools
import math

import jax
import jax.numpy as jnp
from jax import lax
from jax.experimental import pallas as pl
from jax.experimental.pallas import tpu as pltpu
from jax.sharding import PartitionSpec as P

NODES = 8
NEAR = 4
FAR = 4
QUAD = 4
F32 = jnp.float32
BF16 = jnp.bfloat16
MIB = 1 << 20

NEAR_COUNT = NEAR
FAR_LIST = NEAR + 1
FAR_COUNT = FAR_LIST + FAR
LEAF = FAR_COUNT + 1
META = 128
PIECES = 4


def vmem():
    return pl.BlockSpec(memory_space=pltpu.VMEM)


def smem():
    return pl.BlockSpec(memory_space=pltpu.SMEM)


def params():
    return pltpu.CompilerParams(vmem_limit_bytes=24 * MIB)


def norm_column(points, scale):
    wide = points.astype(F32)
    return jnp.sum(wide * wide, axis=1, keepdims=True) * scale


def norm_row(points, scale):
    column = norm_column(points, scale)
    return jnp.transpose(jnp.broadcast_to(column, (column.shape[0], 128)))[0:1, :]


def listed(meta, row, first, count, value):
    hit = jnp.bool_(False)
    for slot in range(count):
        hit = hit | ((meta[row, first + slot] == value) & (slot < meta[row, first + count]))
    return hit


def near_hit(meta, row, leaf):
    return listed(meta, row, 0, NEAR, leaf)


def far_hit(meta, row, node):
    return listed(meta, row, FAR_LIST, FAR, node)


def half_scale(dim):
    return 0.5 * math.log2(math.e) / dim


def kernel_sum(xpts, xsq, ypts, ysq, wts):
    dim = xpts.shape[1]
    scores = lax.dot_general(
        xpts, ypts, (((1,), (1,)), ((), ())), preferred_element_type=F32
    )
    kern = jnp.exp2(scores * (2.0 * half_scale(dim)) - xsq - ysq)
    return jnp.dot(kern.astype(BF16), wts, preferred_element_type=F32)


def call(body, kinds, scalars, arrays, scratch=()):
    return pl.pallas_call(
        body,
        out_shape=kinds,
        in_specs=[smem()] * len(scalars) + [vmem()] * len(arrays),
        out_specs=jax.tree.map(lambda _: vmem(), kinds),
        scratch_shapes=scratch,
        compiler_params=params(),
        cost_estimate=pl.CostEstimate(flops=1000, bytes_accessed=1000, transcendentals=0),
    )(*scalars, *arrays)


def project_body(near_list, near_count, far_list, far_count, wts, proj, keep, meta, *pieces):
    leaf = lax.axis_index("pts")
    core = leaf % 2
    fields = [near_list[0, slot] for slot in range(NEAR)] + [near_count[0]]
    fields += [far_list[0, slot] for slot in range(FAR)] + [far_count[0], leaf]
    lane = lax.broadcasted_iota(jnp.int32, meta.shape, 1)
    row = jnp.zeros(meta.shape, jnp.int32)
    for place, field in enumerate(fields):
        row = jnp.where(lane == place, field, row)
    meta[...] = row
    whole = jnp.dot(proj[...], wts[...], preferred_element_type=F32)
    pairs, count, wcols = keep.shape
    whole = whole.reshape(pairs, 2, count, wcols)
    other = jnp.where(core == 0, whole[:, 1], whole[:, 0])
    keep[...] = jnp.where(core == 0, whole[:, 0], whole[:, 1])
    other = other.reshape(pairs * count, wcols).astype(BF16)
    first = 0
    for piece in pieces:
        piece[...] = other[first : first + piece.shape[0]]
        first += piece.shape[0]


def project(group, lists, wts, proj):
    count, wcols = proj.shape[0] // group, wts.shape[1]
    pairs = group // 2
    piece = jax.ShapeDtypeStruct((pairs * count // PIECES, wcols), BF16)
    kinds = (
        jax.ShapeDtypeStruct((pairs, count, wcols), F32),
        jax.ShapeDtypeStruct((1, META), jnp.int32),
    ) + (piece,) * PIECES
    return call(project_body, kinds, lists, (wts, proj))


def pack_body(idx, pts, keep, got, packed):
    rows, dim = pts.shape
    place = lax.broadcasted_iota(jnp.int32, (rows, idx.shape[1]), 0)
    pick = (place == idx[...]).astype(F32).astype(BF16)
    packed[:, :dim] = lax.dot_general(
        pick, pts[...], (((0,), (0,)), ((), ())), preferred_element_type=F32
    ).astype(BF16)
    packed[:, dim:] = (keep[0] + got[0].astype(F32)).astype(BF16)


def pack(idx, pts, keep, got):
    shape = (idx.shape[1], pts.shape[1] + keep.shape[2])
    return call(pack_body, jax.ShapeDtypeStruct(shape, BF16), (), (idx, pts, keep, got))


def quad_body(group, places, targets, own, meta, *refs):
    packed, refs = refs[: len(places)], refs[len(places) :]
    many = len(targets)
    xpts, refs = refs[:many], refs[many:]
    if own:
        mine, mine_w, *outs = refs
    else:
        start, outs = refs[:many], refs[many:]
    dim = xpts[0].shape[1]
    scale = half_scale(dim)
    quads = lax.axis_size("pts") // QUAD
    leaf = meta[0, LEAF]
    quad = leaf // QUAD
    count = packed[0].shape[0]
    nodes = []
    for turn, flip in places:
        deep = (quad // 2 - turn + quads // 2) % (quads // 2)
        nodes.append((deep * 2 + (quad + flip) % 2) * QUAD // group)
    everything = jnp.concatenate([ref[...] for ref in packed], axis=0)
    ypts, wts = everything[:, :dim], everything[:, dim:]
    ysq = norm_row(ypts, scale)
    if own:
        own_sq = norm_row(mine[...], scale)
    for place, target in enumerate(targets):
        hits = [far_hit(meta, target, node) for node in nodes]
        some = functools.reduce(jnp.logical_or, hits)
        away = [jnp.full((1, count), jnp.where(hit, 0.0, 1e30), F32) for hit in hits]
        far_sq = ysq + jnp.concatenate(away, axis=1)
        xsq = norm_column(xpts[place][...], scale)

        def far(place=place, xsq=xsq, far_sq=far_sq):
            return kernel_sum(xpts[place][...], xsq, ypts, far_sq, wts)

        out = outs[place]
        if own:
            def near(place=place, xsq=xsq):
                return kernel_sum(xpts[place][...], xsq, mine[...], own_sq, mine_w[...])

            if target == 0:
                out[...] = near()
            else:
                hit = near_hit(meta, target, leaf)

                @pl.when(hit)
                def _(out=out, near=near):
                    out[...] = near()

                @pl.when(jnp.logical_not(hit))
                def _(out=out):
                    out[...] = jnp.zeros_like(out)

            @pl.when(some)
            def _(out=out, far=far):
                out[...] += far()
        else:
            @pl.when(some)
            def _(out=out, far=far, place=place):
                out[...] = (start[place][...] + far()).astype(out.dtype)

            @pl.when(jnp.logical_not(some))
            def _(out=out, place=place):
                out[...] = start[place][...].astype(out.dtype)


def quad_terms(group, places, targets, meta, packed, xpts, mine, start, kinds):
    rows = xpts[0].shape[0]
    wcols = packed[0].shape[1] - xpts[0].shape[1]
    body = functools.partial(quad_body, group, tuple(places), targets, bool(mine))
    shapes = tuple(jax.ShapeDtypeStruct((rows, wcols), kind) for kind in kinds)
    return call(body, shapes, (meta,), (*packed, *xpts, *mine, *start))


def sum_body(one, two, out):
    out[...] = (one[...] + two[...].astype(F32)).astype(BF16)


def sum_terms(one, two):
    return call(sum_body, jax.ShapeDtypeStruct(one.shape, BF16), (), (one, two))


def cross_body(meta, own, other, start, start_other, ypts, wts, acc, *halves):
    leaf = meta[0, LEAF]
    away = leaf + 4 * (leaf // 2 % 2) - 2
    scale = half_scale(own.shape[1])
    ysq = norm_row(ypts[...], scale)

    def term(xpts):
        return kernel_sum(xpts[...], norm_column(xpts[...], scale), ypts[...], ysq, wts[...])

    acc[...] = start[...]
    hit = near_hit(meta, 0, away)

    @pl.when(hit)
    def _():
        acc[...] += term(own)

    def put(value):
        first = 0
        for half in halves:
            half[...] = value[first : first + half.shape[0]].astype(BF16)
            first += half.shape[0]

    hit = near_hit(meta, 1, away)

    @pl.when(hit)
    def _():
        put(start_other[...] + term(other))

    @pl.when(jnp.logical_not(hit))
    def _():
        put(start_other[...])


def cross_terms(meta, xpts, start, ypts, wts):
    rows, wcols = start[0].shape
    half = jax.ShapeDtypeStruct((rows // 2, wcols), BF16)
    shapes = (jax.ShapeDtypeStruct((rows, wcols), F32), half, half)
    return call(cross_body, shapes, (meta,), (*xpts, *start, ypts, wts))


def shards(points, weights, node_proj, skel_idx, near_list, near_count, far_list, far_count):
    leaves = lax.axis_size("pts")
    me = lax.axis_index("pts")
    group = leaves // NODES
    quads = leaves // QUAD
    depth = quads // 2

    def move(value, where):
        pairs = [(source, where(source)) for source in range(leaves)]
        return lax.ppermute(value, "pts", [(a, b) for a, b in pairs if b is not None])

    def bit(level):
        return lambda source: source ^ (1 << level)

    def deeper(turn):
        def where(source):
            quad, place = divmod(source, QUAD)
            deep, side = divmod(quad, 2)
            return ((deep + turn) % depth * 2 + side) * QUAD + place

        return where

    def after(values):
        return lax.optimization_barrier(values)

    def along(way):
        def where(source):
            target = source - way * QUAD if source // 2 % 2 else source + way * QUAD
            return target if 0 <= target < leaves else None

        return where

    core, side, row = bit(0), bit(1), bit(2)

    lists = (near_list, near_count, far_list, far_count)
    keep, meta, *give = project(group, lists, weights, node_proj)
    level = 0
    while True:
        got = [move(piece, bit(level)) for piece in give]
        got = jnp.concatenate(got, axis=0).reshape(keep.shape)
        level += 1
        if keep.shape[0] == 1:
            break
        count = keep.shape[0]
        keep = (keep + got.astype(F32)).reshape(count // 2, 2, *keep.shape[1:])
        upper = (me >> level) % 2 == 1
        give = jnp.where(upper, keep[:, 0], keep[:, 1]).astype(BF16)
        give = [give.reshape(-1, give.shape[-1])]
        keep = jnp.where(upper, keep[:, 1], keep[:, 0])
    cross_w = move(weights, along(-1))
    cross_w = [move(half, core) for half in jnp.split(cross_w, 2)]
    got, pts_later = after((got, points))
    packed = pack(skel_idx, points, keep, got)

    up, down = deeper(1), deeper(depth - 1)
    top = depth // 2
    gathered = {(0, 0): packed}
    pts_side = move(pts_later, side)
    pts_core = move(pts_later, core)
    gathered[1, 0] = move(packed, up)
    gathered[0, 1] = move(packed, row)
    gathered, packed, cross_w = after((gathered, packed, cross_w))
    if depth > 2:
        gathered[depth - 1, 0] = move(packed, down)
    gathered[1, 1] = move(gathered[1, 0], row)
    for hop in (core, side):
        meta = jnp.concatenate([meta, move(meta, hop)], axis=0)
    gathered, pts_side, meta = after((gathered, pts_side, meta))
    cross_w = move(move(jnp.concatenate(cross_w, axis=0), side), core)
    cross_p = move(pts_side, along(1))
    pts_both = move(pts_side, core)
    first_places = sorted(set(gathered) - {(1, 1)})
    if depth > 2:
        gathered[depth - 1, 1] = move(gathered[depth - 1, 0], row)
    for flip in range(2):
        for turn in range(2, top + 1):
            gathered[turn, flip] = move(gathered[turn - 1, flip], up)
        for turn in range(depth - 2, top, -1):
            gathered[turn, flip] = move(gathered[turn + 1, flip], down)

    mine = (points, weights)
    near_x = (points, pts_core)
    side_x = (pts_side, pts_both)
    some = [gathered[place] for place in first_places]
    acc0, acc1 = quad_terms(group, first_places, (0, 1), meta, some, near_x, mine, (), (F32, F32))
    acc2, acc3 = quad_terms(group, first_places, (2, 3), meta, some, side_x, mine, (), (F32, F32))
    gathered, acc0, acc1, acc2, acc3 = after((gathered, acc0, acc1, acc2, acc3))

    last_places = sorted(set(gathered) - set(first_places))
    rest = [gathered[place] for place in last_places]
    (out3,) = quad_terms(group, last_places, (3,), meta, rest, (pts_both,), (), (acc3,), (BF16,))
    got3 = move(out3, core)
    (acc2,) = quad_terms(group, last_places, (2,), meta, rest, (pts_side,), (), (acc2,), (F32,))
    last = move(sum_terms(acc2, got3), side)
    acc0, acc1 = quad_terms(
        group, last_places, (0, 1), meta, rest, near_x, (), (acc0, acc1), (F32, F32)
    )
    acc0, *out1 = cross_terms(meta, near_x, (acc0, acc1), cross_p, cross_w)
    extra = jnp.concatenate([move(half, core) for half in out1], axis=0)
    return acc0 + extra.astype(F32) + last.astype(F32)


def solution(mesh):
    in_specs = (
        P("pts", None),
        P("pts", None),
        P(None, "pts"),
        P("pts", None),
        P("pts", None),
        P("pts"),
        P("pts", None),
        P("pts"),
    )
    out_specs = P("pts", None)
    return jax.shard_map(shards, mesh=mesh, in_specs=in_specs, out_specs=out_specs, check_vma=False)
```

```python
import functools
import math

import jax
import jax.numpy as jnp
from jax import lax
from jax.experimental import pallas as pl
from jax.experimental.pallas import tpu as pltpu
from jax.sharding import PartitionSpec as P

NODES = 8
NEAR = 4
FAR = 4
QUAD = 4
F32 = jnp.float32
BF16 = jnp.bfloat16
MIB = 1 << 20

NEAR_COUNT = NEAR
FAR_LIST = NEAR + 1
FAR_COUNT = FAR_LIST + FAR
LEAF = FAR_COUNT + 1
META = 16
CUTS = 4


def vmem():
    return pl.BlockSpec(memory_space=pltpu.VMEM)


def smem():
    return pl.BlockSpec(memory_space=pltpu.SMEM)


def params(limit=24):
    return pltpu.CompilerParams(vmem_limit_bytes=limit * MIB)


def norm_column(points, scale):
    wide = points.astype(F32)
    return jnp.sum(wide * wide, axis=1, keepdims=True) * scale


def norm_row(points, scale):
    column = norm_column(points, scale)
    return jnp.transpose(jnp.broadcast_to(column, (column.shape[0], 128)))[0:1, :]


def listed(meta, row, first, count, value):
    hit = jnp.bool_(False)
    for slot in range(count):
        hit = hit | ((meta[row, first + slot] == value) & (slot < meta[row, first + count]))
    return hit


def near_hit(meta, row, leaf):
    return listed(meta, row, 0, NEAR, leaf)


def far_hit(meta, row, node):
    return listed(meta, row, FAR_LIST, FAR, node)


def half_scale(dim):
    return 0.5 * math.log2(math.e) / dim


def kernel_sum(xpts, xsq, ypts, ysq, wts):
    dim = xpts.shape[1]
    scores = lax.dot_general(
        xpts, ypts, (((1,), (1,)), ((), ())), preferred_element_type=F32
    )
    kern = jnp.exp2(scores * (2.0 * half_scale(dim)) - xsq - ysq)
    return jnp.dot(kern.astype(BF16), wts, preferred_element_type=F32)


def call(body, kinds, scalars, arrays, scratch=(), outside=(), limit=24):
    return pl.pallas_call(
        body,
        out_shape=kinds,
        in_specs=[smem()] * len(scalars)
        + [vmem()] * len(arrays)
        + [pl.BlockSpec(memory_space=pltpu.HBM)] * len(outside),
        out_specs=jax.tree.map(lambda _: vmem(), kinds),
        scratch_shapes=scratch,
        compiler_params=params(limit),
        cost_estimate=pl.CostEstimate(flops=1000, bytes_accessed=1000, transcendentals=0),
    )(*scalars, *arrays, *outside)


def project_body(wts, proj, keep, *outs):
    *gives, wts_here, proj_here, sems = outs
    copies = []
    for source, target in ((wts, wts_here), (proj, proj_here)):
        rows = source.shape[0] // CUTS
        for cut in range(CUTS):
            part = pl.ds(cut * rows, rows)
            copies.append(pltpu.make_async_copy(source.at[part], target.at[part], sems.at[len(copies)]))
    for copy in copies:
        copy.start()
    for copy in copies:
        copy.wait()
    leaf = lax.axis_index("pts")
    groups, count, wcols = keep.shape
    whole = jnp.dot(proj_here[...], wts_here[...], preferred_element_type=F32)
    whole = whole.reshape(groups, QUAD, count, wcols)
    for turn in range(QUAD):
        block = whole[:, QUAD - 1]
        for place in range(QUAD - 1):
            block = jnp.where((leaf ^ turn) % QUAD == place, whole[:, place], block)
        if turn == 0:
            keep[...] = block
        else:
            gives[turn - 1][...] = block.astype(BF16)


def project(group, wts, proj):
    shape = (group // QUAD, proj.shape[0] // group, wts.shape[1])
    kinds = (jax.ShapeDtypeStruct(shape, F32),) + (jax.ShapeDtypeStruct(shape, BF16),) * (QUAD - 1)
    scratch = [
        pltpu.VMEM(wts.shape, BF16),
        pltpu.VMEM(proj.shape, BF16),
        pltpu.SemaphoreType.DMA((2 * CUTS,)),
    ]
    return call(project_body, kinds, (), (), scratch, (wts, proj), 54)


def pack_body(idx, pts, keep, *refs):
    *got, packed = refs
    rows, dim = pts.shape
    place = lax.broadcasted_iota(jnp.int32, (rows, idx.shape[1]), 0)
    pick = (place == idx[...]).astype(F32).astype(BF16)
    packed[:, :dim] = lax.dot_general(
        pick, pts[...], (((0,), (0,)), ((), ())), preferred_element_type=F32
    ).astype(BF16)
    total = keep[0]
    for part in got:
        total = total + part[0].astype(F32)
    packed[:, dim:] = total.astype(BF16)


def pack(idx, pts, keep, got):
    shape = (idx.shape[1], pts.shape[1] + keep.shape[2])
    return call(pack_body, jax.ShapeDtypeStruct(shape, BF16), (), (idx, pts, keep, *got))


def quad_body(group, places, targets, cuts, own, meta, *refs):
    packed, refs = refs[: len(places)], refs[len(places) :]
    many = len(targets)
    xpts = []
    for size in cuts:
        xpts.append(refs[0][...] if size == 1 else jnp.concatenate([ref[...] for ref in refs[:size]], axis=0))
        refs = refs[size:]
    if own:
        mine, mine_w, *outs = refs
    else:
        start, outs = refs[:many], refs[many:]
    dim = xpts[0].shape[1]
    scale = half_scale(dim)
    quads = lax.axis_size("pts") // QUAD
    leaf = meta[0, LEAF]
    quad = leaf // QUAD
    count = packed[0].shape[0]
    nodes = []
    for turn, flip in places:
        deep = (quad // 2 - turn + quads // 2) % (quads // 2)
        nodes.append((deep * 2 + (quad + flip) % 2) * QUAD // group)
    everything = jnp.concatenate([ref[...] for ref in packed], axis=0)
    ypts, wts = everything[:, :dim], everything[:, dim:]
    ysq = norm_row(ypts, scale)
    if own:
        own_sq = norm_row(mine[...], scale)
    for place, target in enumerate(targets):
        hits = [far_hit(meta, target, node) for node in nodes]
        some = functools.reduce(jnp.logical_or, hits)
        away = [jnp.full((1, count), jnp.where(hit, 0.0, 1e30), F32) for hit in hits]
        far_sq = ysq + jnp.concatenate(away, axis=1)
        xsq = norm_column(xpts[place], scale)

        def far(place=place, xsq=xsq, far_sq=far_sq):
            return kernel_sum(xpts[place], xsq, ypts, far_sq, wts)

        out = outs[place]
        if own:
            def near(place=place, xsq=xsq):
                return kernel_sum(xpts[place], xsq, mine[...], own_sq, mine_w[...])

            if target == 0:
                out[...] = near()
            else:
                hit = near_hit(meta, target, leaf)

                @pl.when(hit)
                def _(out=out, near=near):
                    out[...] = near()

                @pl.when(jnp.logical_not(hit))
                def _(out=out):
                    out[...] = jnp.zeros_like(out)

            @pl.when(some)
            def _(out=out, far=far):
                out[...] += far()
        else:
            @pl.when(some)
            def _(out=out, far=far, place=place):
                out[...] = (start[place][...] + far()).astype(out.dtype)

            @pl.when(jnp.logical_not(some))
            def _(out=out, place=place):
                out[...] = start[place][...].astype(out.dtype)


def quad_terms(group, places, targets, meta, packed, xpts, mine, start, kinds):
    rows = sum(part.shape[0] for part in xpts[0])
    wcols = packed[0].shape[1] - xpts[0][0].shape[1]
    cuts = tuple(len(parts) for parts in xpts)
    body = functools.partial(quad_body, group, tuple(places), targets, cuts, bool(mine))
    shapes = tuple(jax.ShapeDtypeStruct((rows, wcols), kind) for kind in kinds)
    return call(body, shapes, (meta,), (*packed, *sum(xpts, ()), *mine, *start))


def sum_body(one, two, out):
    out[...] = (one[...] + two[...].astype(F32)).astype(BF16)


def sum_terms(one, two):
    return call(sum_body, jax.ShapeDtypeStruct(one.shape, BF16), (), (one, two))


def cross_body(row, meta, xpts, start, ypts, wts, *outs):
    leaf = meta[0, LEAF]
    scale = half_scale(xpts.shape[1])
    hit = near_hit(meta, row, leaf + 4 * (leaf // 2 % 2) - 2)

    def put(value):
        first = 0
        for out in outs:
            out[...] = value[first : first + out.shape[0]].astype(out.dtype)
            first += out.shape[0]

    @pl.when(hit)
    def _():
        xsq, ysq = norm_column(xpts[...], scale), norm_row(ypts[...], scale)
        put(start[...] + kernel_sum(xpts[...], xsq, ypts[...], ysq, wts[...]))

    @pl.when(jnp.logical_not(hit))
    def _():
        put(start[...])


def cross_terms(row, meta, xpts, start, ypts, wts, kind, cuts):
    rows, wcols = start.shape
    shapes = (jax.ShapeDtypeStruct((rows // cuts, wcols), kind),) * cuts
    return call(functools.partial(cross_body, row), shapes, (meta,), (xpts, start, ypts, wts))


def shards(points, weights, node_proj, skel_idx, near_list, near_count, far_list, far_count):
    leaves = lax.axis_size("pts")
    me = lax.axis_index("pts")
    group = leaves // NODES
    quads = leaves // QUAD
    depth = quads // 2

    def move(value, where):
        pairs = [(source, where(source)) for source in range(leaves)]
        return lax.ppermute(value, "pts", [(a, b) for a, b in pairs if b is not None])

    def bit(level):
        return lambda source: source ^ (1 << level)

    def deeper(turn):
        def where(source):
            quad, place = divmod(source, QUAD)
            deep, side = divmod(quad, 2)
            return ((deep + turn) % depth * 2 + side) * QUAD + place

        return where

    def after(values):
        return lax.optimization_barrier(values)

    def along(way):
        def where(source):
            target = source - way * QUAD if source // 2 % 2 else source + way * QUAD
            return target if 0 <= target < leaves else None

        return where

    core, side, row = bit(0), bit(1), bit(2)

    keep, *give = project(group, weights, node_proj)
    got = [move(block, lambda source, turn=turn: source ^ turn) for turn, block in enumerate(give, 1)]
    level = 2
    while keep.shape[0] > 1:
        for part in got:
            keep = keep + part.astype(F32)
        count = keep.shape[0]
        keep = keep.reshape(count // 2, 2, *keep.shape[1:])
        upper = (me >> level) % 2 == 1
        give = jnp.where(upper, keep[:, 0], keep[:, 1]).astype(BF16)
        keep = jnp.where(upper, keep[:, 1], keep[:, 0])
        got = [move(give, bit(level))]
        level += 1
    cross_w = move(weights, along(-1))
    cut = weights.shape[0] * 11 // 256 * 16
    cross_w = [move(part, core) for part in jnp.split(cross_w, [cut])]
    got, pts_later = after((got, points))
    packed = pack(skel_idx, points, keep, got)

    up, down = deeper(1), deeper(depth - 1)
    top = depth // 2
    gathered = {(0, 0): packed}
    pts_side = move(pts_later, side)
    pts_core = move(pts_later, core)
    gathered[1, 0] = move(packed, up)
    gathered[0, 1] = move(packed, row)
    gathered, packed, cross_w = after((gathered, packed, cross_w))
    if depth > 2:
        gathered[depth - 1, 0] = move(packed, down)
    gathered[1, 1] = move(gathered[1, 0], row)
    meta = [near_list[0], near_count, far_list[0], far_count, me[None]]
    meta = jnp.concatenate(meta + [jnp.zeros((META - LEAF - 1,), jnp.int32)])[None]
    for hop in (core, side):
        meta = jnp.concatenate([meta, move(meta, hop)], axis=0)
    gathered, pts_side, meta = after((gathered, pts_side, meta))
    cross_w = move(move(jnp.concatenate(cross_w, axis=0), side), core)
    cross_p = move(pts_side, along(1))
    pts_both = (move(pts_side, core),)
    first_places = sorted(set(gathered) - {(1, 1)})
    if depth > 2:
        gathered[depth - 1, 1] = move(gathered[depth - 1, 0], row)
    for flip in range(2):
        for turn in range(2, top + 1):
            gathered[turn, flip] = move(gathered[turn - 1, flip], up)
        for turn in range(depth - 2, top, -1):
            gathered[turn, flip] = move(gathered[turn + 1, flip], down)

    mine = (points, weights)
    near_x = ((points,), (pts_core,))
    side_x = ((pts_side,), pts_both)
    some = [gathered[place] for place in first_places]
    acc0, acc1 = quad_terms(group, first_places, (0, 1), meta, some, near_x, mine, (), (F32, F32))
    acc2, acc3 = quad_terms(group, first_places, (2, 3), meta, some, side_x, mine, (), (F32, F32))
    gathered, acc0, acc1, acc2, acc3 = after((gathered, acc0, acc1, acc2, acc3))

    last_places = sorted(set(gathered) - set(first_places))
    rest = [gathered[place] for place in last_places]
    (out3,) = quad_terms(group, last_places, (3,), meta, rest, (pts_both,), (), (acc3,), (BF16,))
    got3 = move(out3, core)
    (acc2,) = quad_terms(group, last_places, (2,), meta, rest, ((pts_side,),), (), (acc2,), (F32,))
    last = move(sum_terms(acc2, got3), side)
    acc0, acc1 = quad_terms(
        group, last_places, (0, 1), meta, rest, near_x, (), (acc0, acc1), (F32, F32)
    )
    out1 = cross_terms(1, meta, pts_core, acc1, cross_p, cross_w, BF16, 2)
    (acc0,) = cross_terms(0, meta, points, acc0, cross_p, cross_w, F32, 1)
    extra = jnp.concatenate([move(half, core) for half in out1], axis=0)
    return acc0 + extra.astype(F32) + last.astype(F32)


def solution(mesh):
    in_specs = (
        P("pts", None),
        P("pts", None),
        P(None, "pts"),
        P("pts", None),
        P("pts", None),
        P("pts"),
        P("pts", None),
        P("pts"),
    )
    out_specs = P("pts", None)
    return jax.shard_map(shards, mesh=mesh, in_specs=in_specs, out_specs=out_specs, check_vma=False)
```

```python
import functools
import math

import jax
import jax.numpy as jnp
from jax import lax
from jax.experimental import pallas as pl
from jax.experimental.pallas import tpu as pltpu
from jax.sharding import PartitionSpec as P

NODES = 8
NEAR = 4
FAR = 4
QUAD = 4
F32 = jnp.float32
BF16 = jnp.bfloat16
MIB = 1 << 20

NEAR_COUNT = NEAR
FAR_LIST = NEAR + 1
FAR_COUNT = FAR_LIST + FAR
LEAF = FAR_COUNT + 1
META = 16


def vmem():
    return pl.BlockSpec(memory_space=pltpu.VMEM)


def smem():
    return pl.BlockSpec(memory_space=pltpu.SMEM)


def params():
    return pltpu.CompilerParams(vmem_limit_bytes=16 * MIB)


def norm_column(points, scale):
    wide = points.astype(F32)
    return jnp.sum(wide * wide, axis=1, keepdims=True) * scale


def norm_row(points, scale):
    column = norm_column(points, scale)
    return jnp.transpose(jnp.broadcast_to(column, (column.shape[0], 128)))[0:1, :]


def listed(meta, row, first, count, value):
    hit = jnp.bool_(False)
    for slot in range(count):
        hit = hit | ((meta[row, first + slot] == value) & (slot < meta[row, first + count]))
    return hit


def near_hit(meta, row, leaf):
    return listed(meta, row, 0, NEAR, leaf)


def far_hit(meta, row, node):
    return listed(meta, row, FAR_LIST, FAR, node)


def half_scale(dim):
    return 0.5 * math.log2(math.e) / dim


def kernel_sum(xpts, xsq, ypts, ysq, wts):
    dim = xpts.shape[1]
    scores = lax.dot_general(
        xpts, ypts, (((1,), (1,)), ((), ())), preferred_element_type=F32
    )
    kern = jnp.exp2(scores * (2.0 * half_scale(dim)) - xsq - ysq)
    return jnp.dot(kern.astype(BF16), wts, preferred_element_type=F32)


def call(body, kinds, scalars, arrays):
    return pl.pallas_call(
        body,
        out_shape=kinds,
        in_specs=[smem()] * len(scalars)
        + [vmem()] * len(arrays),
        out_specs=jax.tree.map(lambda _: vmem(), kinds),
        compiler_params=params(),
        cost_estimate=pl.CostEstimate(flops=1000, bytes_accessed=1000, transcendentals=0),
    )(*scalars, *arrays)


def project_body(wts, proj, keep, *gives):
    leaf = lax.axis_index("pts")
    groups, count, wcols = keep.shape
    whole = jnp.dot(proj[...], wts[...], preferred_element_type=F32)
    whole = whole.reshape(groups, QUAD, count, wcols)
    for turn in range(QUAD):
        block = whole[:, QUAD - 1]
        for place in range(QUAD - 1):
            block = jnp.where((leaf ^ turn) % QUAD == place, whole[:, place], block)
        if turn == 0:
            keep[...] = block
        else:
            gives[turn - 1][...] = block.astype(BF16)


def project(group, wts, proj):
    shape = (group // QUAD, proj.shape[0] // group, wts.shape[1])
    kinds = (jax.ShapeDtypeStruct(shape, F32),) + (jax.ShapeDtypeStruct(shape, BF16),) * (QUAD - 1)
    return call(project_body, kinds, (), (wts, proj))


def pack_body(idx, pts, keep, *refs):
    *got, packed = refs
    rows, dim = pts.shape
    place = lax.broadcasted_iota(jnp.int32, (rows, idx.shape[1]), 0)
    pick = (place == idx[...]).astype(F32).astype(BF16)
    packed[:, :dim] = lax.dot_general(
        pick, pts[...], (((0,), (0,)), ((), ())), preferred_element_type=F32
    ).astype(BF16)
    total = keep[0]
    for part in got:
        total = total + part[0].astype(F32)
    packed[:, dim:] = total.astype(BF16)


def pack(idx, pts, keep, got):
    shape = (idx.shape[1], pts.shape[1] + keep.shape[2])
    return call(pack_body, jax.ShapeDtypeStruct(shape, BF16), (), (idx, pts, keep, *got))


def quad_body(group, places, targets, cuts, own, meta, *refs):
    packed, refs = refs[: len(places)], refs[len(places) :]
    many = len(targets)
    xpts = []
    for size in cuts:
        xpts.append(refs[0][...] if size == 1 else jnp.concatenate([ref[...] for ref in refs[:size]], axis=0))
        refs = refs[size:]
    if own:
        mine, mine_w, *outs = refs
    else:
        start, outs = refs[:many], refs[many:]
    dim = xpts[0].shape[1]
    scale = half_scale(dim)
    quads = lax.axis_size("pts") // QUAD
    leaf = meta[0, LEAF]
    quad = leaf // QUAD
    count = packed[0].shape[0]
    nodes = []
    for turn, flip in places:
        deep = (quad // 2 - turn + quads // 2) % (quads // 2)
        nodes.append((deep * 2 + (quad + flip) % 2) * QUAD // group)
    everything = jnp.concatenate([ref[...] for ref in packed], axis=0)
    ypts, wts = everything[:, :dim], everything[:, dim:]
    ysq = norm_row(ypts, scale)
    if own:
        own_sq = norm_row(mine[...], scale)
    for place, target in enumerate(targets):
        hits = [far_hit(meta, target, node) for node in nodes]
        some = functools.reduce(jnp.logical_or, hits)
        away = [jnp.full((1, count), jnp.where(hit, 0.0, 1e30), F32) for hit in hits]
        far_sq = ysq + jnp.concatenate(away, axis=1)
        xsq = norm_column(xpts[place], scale)

        def far(place=place, xsq=xsq, far_sq=far_sq):
            return kernel_sum(xpts[place], xsq, ypts, far_sq, wts)

        out = outs[place]
        if own:
            def near(place=place, xsq=xsq):
                return kernel_sum(xpts[place], xsq, mine[...], own_sq, mine_w[...])

            if target == 0:
                out[...] = near()
            else:
                hit = near_hit(meta, target, leaf)

                @pl.when(hit)
                def _(out=out, near=near):
                    out[...] = near()

                @pl.when(jnp.logical_not(hit))
                def _(out=out):
                    out[...] = jnp.zeros_like(out)

            @pl.when(some)
            def _(out=out, far=far):
                out[...] += far()
        else:
            @pl.when(some)
            def _(out=out, far=far, place=place):
                out[...] = (start[place][...] + far()).astype(out.dtype)

            @pl.when(jnp.logical_not(some))
            def _(out=out, place=place):
                out[...] = start[place][...].astype(out.dtype)


def quad_terms(group, places, targets, meta, packed, xpts, mine, start, kinds):
    rows = sum(part.shape[0] for part in xpts[0])
    wcols = packed[0].shape[1] - xpts[0][0].shape[1]
    cuts = tuple(len(parts) for parts in xpts)
    body = functools.partial(quad_body, group, tuple(places), targets, cuts, bool(mine))
    shapes = tuple(jax.ShapeDtypeStruct((rows, wcols), kind) for kind in kinds)
    return call(body, shapes, (meta,), (*packed, *sum(xpts, ()), *mine, *start))


def sum_body(one, two, out):
    out[...] = (one[...] + two[...].astype(F32)).astype(BF16)


def sum_terms(one, two):
    return call(sum_body, jax.ShapeDtypeStruct(one.shape, BF16), (), (one, two))


def cross_body(row, meta, xpts, start, ypts, wts, *outs):
    leaf = meta[0, LEAF]
    scale = half_scale(xpts.shape[1])
    hit = near_hit(meta, row, leaf + 4 * (leaf // 2 % 2) - 2)

    def put(value):
        first = 0
        for out in outs:
            out[...] = value[first : first + out.shape[0]].astype(out.dtype)
            first += out.shape[0]

    @pl.when(hit)
    def _():
        xsq, ysq = norm_column(xpts[...], scale), norm_row(ypts[...], scale)
        put(start[...] + kernel_sum(xpts[...], xsq, ypts[...], ysq, wts[...]))

    @pl.when(jnp.logical_not(hit))
    def _():
        put(start[...])


def cross_terms(row, meta, xpts, start, ypts, wts, kind, cuts):
    rows, wcols = start.shape
    shapes = (jax.ShapeDtypeStruct((rows // cuts, wcols), kind),) * cuts
    return call(functools.partial(cross_body, row), shapes, (meta,), (xpts, start, ypts, wts))


def shards(points, weights, node_proj, skel_idx, near_list, near_count, far_list, far_count):
    leaves = lax.axis_size("pts")
    me = lax.axis_index("pts")
    group = leaves // NODES
    quads = leaves // QUAD
    depth = quads // 2

    def move(value, where):
        pairs = [(source, where(source)) for source in range(leaves)]
        return lax.ppermute(value, "pts", [(a, b) for a, b in pairs if b is not None])

    def bit(level):
        return lambda source: source ^ (1 << level)

    def deeper(turn):
        def where(source):
            quad, place = divmod(source, QUAD)
            deep, side = divmod(quad, 2)
            return ((deep + turn) % depth * 2 + side) * QUAD + place

        return where

    def after(values):
        return lax.optimization_barrier(values)

    def along(way):
        def where(source):
            target = source - way * QUAD if source // 2 % 2 else source + way * QUAD
            return target if 0 <= target < leaves else None

        return where

    core, side, row = bit(0), bit(1), bit(2)

    keep, *give = project(group, weights, node_proj)
    got = [move(block, lambda source, turn=turn: source ^ turn) for turn, block in enumerate(give, 1)]
    level = 2
    while keep.shape[0] > 1:
        for part in got:
            keep = keep + part.astype(F32)
        count = keep.shape[0]
        keep = keep.reshape(count // 2, 2, *keep.shape[1:])
        upper = (me >> level) % 2 == 1
        give = jnp.where(upper, keep[:, 0], keep[:, 1]).astype(BF16)
        keep = jnp.where(upper, keep[:, 1], keep[:, 0])
        got = [move(give, bit(level))]
        level += 1
    cross_w = move(weights, along(-1))
    cut = weights.shape[0] * 11 // 256 * 16
    cross_w = [move(part, core) for part in jnp.split(cross_w, [cut])]
    got, pts_later = after((got, points))
    packed = pack(skel_idx, points, keep, got)

    up, down = deeper(1), deeper(depth - 1)
    top = depth // 2
    gathered = {(0, 0): packed}
    pts_side = move(pts_later, side)
    pts_core = move(pts_later, core)
    gathered[1, 0] = move(packed, up)
    gathered[0, 1] = move(packed, row)
    gathered, packed, cross_w = after((gathered, packed, cross_w))
    if depth > 2:
        gathered[depth - 1, 0] = move(packed, down)
    gathered[1, 1] = move(gathered[1, 0], row)
    meta = [near_list[0], near_count, far_list[0], far_count, me[None]]
    meta = jnp.concatenate(meta + [jnp.zeros((META - LEAF - 1,), jnp.int32)])[None]
    for hop in (core, side):
        meta = jnp.concatenate([meta, move(meta, hop)], axis=0)
    gathered, pts_side, meta = after((gathered, pts_side, meta))
    cross_w = move(move(jnp.concatenate(cross_w, axis=0), side), core)
    cross_p = move(pts_side, along(1))
    pts_both = (move(pts_side, core),)
    first_places = sorted(set(gathered) - {(1, 1)})
    if depth > 2:
        gathered[depth - 1, 1] = move(gathered[depth - 1, 0], row)
    for flip in range(2):
        for turn in range(2, top + 1):
            gathered[turn, flip] = move(gathered[turn - 1, flip], up)
        for turn in range(depth - 2, top, -1):
            gathered[turn, flip] = move(gathered[turn + 1, flip], down)

    mine = (points, weights)
    near_x = ((points,), (pts_core,))
    side_x = ((pts_side,), pts_both)
    some = [gathered[place] for place in first_places]
    acc0, acc1 = quad_terms(group, first_places, (0, 1), meta, some, near_x, mine, (), (F32, F32))
    acc2, acc3 = quad_terms(group, first_places, (2, 3), meta, some, side_x, mine, (), (F32, F32))
    gathered, acc0, acc1, acc2, acc3 = after((gathered, acc0, acc1, acc2, acc3))

    last_places = sorted(set(gathered) - set(first_places))
    rest = [gathered[place] for place in last_places]
    (out3,) = quad_terms(group, last_places, (3,), meta, rest, (pts_both,), (), (acc3,), (BF16,))
    got3 = move(out3, core)
    (acc2,) = quad_terms(group, last_places, (2,), meta, rest, ((pts_side,),), (), (acc2,), (F32,))
    last = move(sum_terms(acc2, got3), side)
    acc0, acc1 = quad_terms(
        group, last_places, (0, 1), meta, rest, near_x, (), (acc0, acc1), (F32, F32)
    )
    out1 = cross_terms(1, meta, pts_core, acc1, cross_p, cross_w, BF16, 2)
    (acc0,) = cross_terms(0, meta, points, acc0, cross_p, cross_w, F32, 1)
    extra = jnp.concatenate([move(half, core) for half in out1], axis=0)
    return acc0 + extra.astype(F32) + last.astype(F32)


def solution(mesh):
    in_specs = (
        P("pts", None),
        P("pts", None),
        P(None, "pts"),
        P("pts", None),
        P("pts", None),
        P("pts"),
        P("pts", None),
        P("pts"),
    )
    out_specs = P("pts", None)
    return jax.shard_map(shards, mesh=mesh, in_specs=in_specs, out_specs=out_specs, check_vma=False)
```

```python
import functools
import math

import jax
import jax.numpy as jnp
from jax import lax
from jax.experimental import pallas as pl
from jax.experimental.pallas import tpu as pltpu
from jax.sharding import PartitionSpec as P

NODES = 8
NEAR = 4
FAR = 4
QUAD = 4
F32 = jnp.float32
BF16 = jnp.bfloat16
MIB = 1 << 20

NEAR_COUNT = NEAR
FAR_LIST = NEAR + 1
FAR_COUNT = FAR_LIST + FAR
LEAF = FAR_COUNT + 1
META = 16
PIECES = 4


def vmem():
    return pl.BlockSpec(memory_space=pltpu.VMEM)


def smem():
    return pl.BlockSpec(memory_space=pltpu.SMEM)


def params():
    return pltpu.CompilerParams(vmem_limit_bytes=16 * MIB)


def norm_column(points, scale):
    wide = points.astype(F32)
    return jnp.sum(wide * wide, axis=1, keepdims=True) * scale


def norm_row(points, scale):
    column = norm_column(points, scale)
    return jnp.transpose(jnp.broadcast_to(column, (column.shape[0], 128)))[0:1, :]


def listed(meta, row, first, count, value):
    hit = jnp.bool_(False)
    for slot in range(count):
        hit = hit | ((meta[row, first + slot] == value) & (slot < meta[row, first + count]))
    return hit


def near_hit(meta, row, leaf):
    return listed(meta, row, 0, NEAR, leaf)


def far_hit(meta, row, node):
    return listed(meta, row, FAR_LIST, FAR, node)


def half_scale(dim):
    return 0.5 * math.log2(math.e) / dim


def kernel_sum(xpts, xsq, ypts, ysq, wts):
    dim = xpts.shape[1]
    scores = lax.dot_general(
        xpts, ypts, (((1,), (1,)), ((), ())), preferred_element_type=F32
    )
    kern = jnp.exp2(scores * (2.0 * half_scale(dim)) - xsq - ysq)
    return jnp.dot(kern.astype(BF16), wts, preferred_element_type=F32)


def call(body, kinds, scalars, arrays):
    return pl.pallas_call(
        body,
        out_shape=kinds,
        in_specs=[smem()] * len(scalars)
        + [vmem()] * len(arrays),
        out_specs=jax.tree.map(lambda _: vmem(), kinds),
        compiler_params=params(),
        cost_estimate=pl.CostEstimate(flops=1000, bytes_accessed=1000, transcendentals=0),
    )(*scalars, *arrays)


def project_body(wts, proj, keep, *gives):
    leaf = lax.axis_index("pts")
    groups, count, wcols = keep.shape
    whole = jnp.dot(proj[...], wts[...], preferred_element_type=F32)
    whole = whole.reshape(groups, QUAD, count, wcols)
    for turn in range(QUAD):
        block = whole[:, QUAD - 1]
        for place in range(QUAD - 1):
            block = jnp.where((leaf ^ turn) % QUAD == place, whole[:, place], block)
        if turn == 0:
            keep[...] = block
        else:
            gives[turn - 1][...] = block.astype(BF16)


def project(group, wts, proj):
    shape = (group // QUAD, proj.shape[0] // group, wts.shape[1])
    kinds = (jax.ShapeDtypeStruct(shape, F32),) + (jax.ShapeDtypeStruct(shape, BF16),) * (QUAD - 1)
    return call(project_body, kinds, (), (wts, proj))


def pack_body(idx, pts, keep, *refs):
    *got, packed = refs
    rows, dim = pts.shape
    place = lax.broadcasted_iota(jnp.int32, (rows, idx.shape[1]), 0)
    pick = (place == idx[...]).astype(F32).astype(BF16)
    packed[:, :dim] = lax.dot_general(
        pick, pts[...], (((0,), (0,)), ((), ())), preferred_element_type=F32
    ).astype(BF16)
    total = keep[0]
    for part in got:
        total = total + part[0].astype(F32)
    packed[:, dim:] = total.astype(BF16)


def pack(idx, pts, keep, got):
    shape = (idx.shape[1], pts.shape[1] + keep.shape[2])
    return call(pack_body, jax.ShapeDtypeStruct(shape, BF16), (), (idx, pts, keep, *got))


def quad_body(group, places, targets, cuts, own, meta, *refs):
    packed, refs = refs[: len(places)], refs[len(places) :]
    many = len(targets)
    xpts = []
    for size in cuts:
        xpts.append(refs[0][...] if size == 1 else jnp.concatenate([ref[...] for ref in refs[:size]], axis=0))
        refs = refs[size:]
    if own:
        mine, mine_w, *outs = refs
    else:
        start, outs = refs[:many], refs[many:]
    dim = xpts[0].shape[1]
    scale = half_scale(dim)
    quads = lax.axis_size("pts") // QUAD
    leaf = meta[0, LEAF]
    quad = leaf // QUAD
    count = packed[0].shape[0]
    nodes = []
    for turn, flip in places:
        deep = (quad // 2 - turn + quads // 2) % (quads // 2)
        nodes.append((deep * 2 + (quad + flip) % 2) * QUAD // group)
    everything = jnp.concatenate([ref[...] for ref in packed], axis=0)
    ypts, wts = everything[:, :dim], everything[:, dim:]
    ysq = norm_row(ypts, scale)
    if own:
        own_sq = norm_row(mine[...], scale)
    for place, target in enumerate(targets):
        hits = [far_hit(meta, target, node) for node in nodes]
        some = functools.reduce(jnp.logical_or, hits)
        away = [jnp.full((1, count), jnp.where(hit, 0.0, 1e30), F32) for hit in hits]
        far_sq = ysq + jnp.concatenate(away, axis=1)
        xsq = norm_column(xpts[place], scale)

        def far(place=place, xsq=xsq, far_sq=far_sq):
            return kernel_sum(xpts[place], xsq, ypts, far_sq, wts)

        out = outs[place]
        if own:
            def near(place=place, xsq=xsq):
                return kernel_sum(xpts[place], xsq, mine[...], own_sq, mine_w[...])

            if target == 0:
                out[...] = near()
            else:
                hit = near_hit(meta, target, leaf)

                @pl.when(hit)
                def _(out=out, near=near):
                    out[...] = near()

                @pl.when(jnp.logical_not(hit))
                def _(out=out):
                    out[...] = jnp.zeros_like(out)

            @pl.when(some)
            def _(out=out, far=far):
                out[...] += far()
        else:
            @pl.when(some)
            def _(out=out, far=far, place=place):
                out[...] = (start[place][...] + far()).astype(out.dtype)

            @pl.when(jnp.logical_not(some))
            def _(out=out, place=place):
                out[...] = start[place][...].astype(out.dtype)


def quad_terms(group, places, targets, meta, packed, xpts, mine, start, kinds):
    rows = sum(part.shape[0] for part in xpts[0])
    wcols = packed[0].shape[1] - xpts[0][0].shape[1]
    cuts = tuple(len(parts) for parts in xpts)
    body = functools.partial(quad_body, group, tuple(places), targets, cuts, bool(mine))
    shapes = tuple(jax.ShapeDtypeStruct((rows, wcols), kind) for kind in kinds)
    return call(body, shapes, (meta,), (*packed, *sum(xpts, ()), *mine, *start))


def sum_body(one, two, out):
    out[...] = (one[...] + two[...].astype(F32)).astype(BF16)


def sum_terms(one, two):
    return call(sum_body, jax.ShapeDtypeStruct(one.shape, BF16), (), (one, two))


def cross_body(row, more, meta, xpts, start, ypts, wts, *refs):
    extras, outs = refs[:more], refs[more:]
    leaf = meta[0, LEAF]
    scale = half_scale(xpts.shape[1])
    hit = near_hit(meta, row, leaf + 4 * (leaf // 2 % 2) - 2)

    def put(value):
        for extra in extras:
            value = value + extra[...].astype(F32)
        first = 0
        for out in outs:
            out[...] = value[first : first + out.shape[0]].astype(out.dtype)
            first += out.shape[0]

    @pl.when(hit)
    def _():
        xsq, ysq = norm_column(xpts[...], scale), norm_row(ypts[...], scale)
        put(start[...] + kernel_sum(xpts[...], xsq, ypts[...], ysq, wts[...]))

    @pl.when(jnp.logical_not(hit))
    def _():
        put(start[...])


def cross_terms(row, meta, xpts, start, ypts, wts, kind, cuts, extras=()):
    rows, wcols = start.shape
    shapes = (jax.ShapeDtypeStruct((rows // cuts, wcols), kind),) * cuts
    body = functools.partial(cross_body, row, len(extras))
    return call(body, shapes, (meta,), (xpts, start, ypts, wts, *extras))


def finish_body(acc, upper, lower, out, here, sems):
    rows = acc.shape[0] // PIECES
    copies = []
    for piece in range(PIECES):
        part = pl.ds(piece * rows, rows)
        half, first = divmod(piece * rows, upper.shape[0])
        other = (upper, lower)[half][first : first + rows]
        here[part, :] = acc[part, :] + other.astype(F32)
        copy = pltpu.make_async_copy(here.at[part], out.at[part], sems.at[piece])
        copy.start()
        copies.append(copy)
    for copy in copies:
        copy.wait()


def finish(acc, upper, lower):
    return pl.pallas_call(
        finish_body,
        out_shape=jax.ShapeDtypeStruct(acc.shape, F32),
        in_specs=[vmem()] * 3,
        out_specs=pl.BlockSpec(memory_space=pl.ANY),
        scratch_shapes=[pltpu.VMEM(acc.shape, F32), pltpu.SemaphoreType.DMA((PIECES,))],
        compiler_params=params(),
        cost_estimate=pl.CostEstimate(flops=1000, bytes_accessed=1000, transcendentals=0),
    )(acc, upper, lower)


def shards(points, weights, node_proj, skel_idx, near_list, near_count, far_list, far_count):
    leaves = lax.axis_size("pts")
    me = lax.axis_index("pts")
    group = leaves // NODES
    quads = leaves // QUAD
    depth = quads // 2

    def move(value, where):
        pairs = [(source, where(source)) for source in range(leaves)]
        return lax.ppermute(value, "pts", [(a, b) for a, b in pairs if b is not None])

    def bit(level):
        return lambda source: source ^ (1 << level)

    def deeper(turn):
        def where(source):
            quad, place = divmod(source, QUAD)
            deep, side = divmod(quad, 2)
            return ((deep + turn) % depth * 2 + side) * QUAD + place

        return where

    def after(values):
        return lax.optimization_barrier(values)

    def along(way):
        def where(source):
            target = source - way * QUAD if source // 2 % 2 else source + way * QUAD
            return target if 0 <= target < leaves else None

        return where

    core, side, row = bit(0), bit(1), bit(2)

    keep, *give = project(group, weights, node_proj)
    got = [move(block, lambda source, turn=turn: source ^ turn) for turn, block in enumerate(give, 1)]
    level = 2
    while keep.shape[0] > 1:
        for part in got:
            keep = keep + part.astype(F32)
        count = keep.shape[0]
        keep = keep.reshape(count // 2, 2, *keep.shape[1:])
        upper = (me >> level) % 2 == 1
        give = jnp.where(upper, keep[:, 0], keep[:, 1]).astype(BF16)
        keep = jnp.where(upper, keep[:, 1], keep[:, 0])
        got = [move(give, bit(level))]
        level += 1
    cross_w = move(weights, along(-1))
    cut = weights.shape[0] * 11 // 256 * 16
    cross_w = [move(part, core) for part in jnp.split(cross_w, [cut])]
    got, pts_later = after((got, points))
    packed = pack(skel_idx, points, keep, got)

    up, down = deeper(1), deeper(depth - 1)
    top = depth // 2
    gathered = {(0, 0): packed}
    pts_side = move(pts_later, side)
    pts_core = move(pts_later, core)
    gathered[1, 0] = move(packed, up)
    gathered[0, 1] = move(packed, row)
    gathered, packed, cross_w = after((gathered, packed, cross_w))
    if depth > 2:
        gathered[depth - 1, 0] = move(packed, down)
    gathered[1, 1] = move(gathered[1, 0], row)
    meta = [near_list[0], near_count, far_list[0], far_count, me[None]]
    meta = jnp.concatenate(meta + [jnp.zeros((META - LEAF - 1,), jnp.int32)])[None]
    for hop in (core, side):
        meta = jnp.concatenate([meta, move(meta, hop)], axis=0)
    gathered, pts_side, meta = after((gathered, pts_side, meta))
    cross_w = move(move(jnp.concatenate(cross_w, axis=0), side), core)
    cross_p = move(pts_side, along(1))
    pts_both = (move(pts_side, core),)
    first_places = sorted(set(gathered) - {(1, 1)})
    if depth > 2:
        gathered[depth - 1, 1] = move(gathered[depth - 1, 0], row)
    for flip in range(2):
        for turn in range(2, top + 1):
            gathered[turn, flip] = move(gathered[turn - 1, flip], up)
        for turn in range(depth - 2, top, -1):
            gathered[turn, flip] = move(gathered[turn + 1, flip], down)

    mine = (points, weights)
    near_x = ((points,), (pts_core,))
    side_x = ((pts_side,), pts_both)
    some = [gathered[place] for place in first_places]
    acc0, acc1 = quad_terms(group, first_places, (0, 1), meta, some, near_x, mine, (), (F32, F32))
    acc2, acc3 = quad_terms(group, first_places, (2, 3), meta, some, side_x, mine, (), (F32, F32))
    gathered, acc0, acc1, acc2, acc3 = after((gathered, acc0, acc1, acc2, acc3))

    last_places = sorted(set(gathered) - set(first_places))
    rest = [gathered[place] for place in last_places]
    (out3,) = quad_terms(group, last_places, (3,), meta, rest, (pts_both,), (), (acc3,), (BF16,))
    got3 = move(out3, core)
    (acc2,) = quad_terms(group, last_places, (2,), meta, rest, ((pts_side,),), (), (acc2,), (F32,))
    last = move(sum_terms(acc2, got3), side)
    acc0, acc1 = quad_terms(
        group, last_places, (0, 1), meta, rest, near_x, (), (acc0, acc1), (F32, F32)
    )
    out1 = cross_terms(1, meta, pts_core, acc1, cross_p, cross_w, BF16, 2)
    (acc0,) = cross_terms(0, meta, points, acc0, cross_p, cross_w, F32, 1, (last,))
    return finish(acc0, *[move(half, core) for half in out1])


def solution(mesh):
    in_specs = (
        P("pts", None),
        P("pts", None),
        P(None, "pts"),
        P("pts", None),
        P("pts", None),
        P("pts"),
        P("pts", None),
        P("pts"),
    )
    out_specs = P("pts", None)
    return jax.shard_map(shards, mesh=mesh, in_specs=in_specs, out_specs=out_specs, check_vma=False)
```

```python
import functools
import math

import jax
import jax.numpy as jnp
from jax import lax
from jax.experimental import pallas as pl
from jax.experimental.pallas import tpu as pltpu
from jax.sharding import PartitionSpec as P

NODES = 8
NEAR = 4
FAR = 4
QUAD = 4
F32 = jnp.float32
BF16 = jnp.bfloat16
MIB = 1 << 20

NEAR_COUNT = NEAR
FAR_LIST = NEAR + 1
FAR_COUNT = FAR_LIST + FAR
LEAF = FAR_COUNT + 1
META = 16
PIECES = 8


def vmem():
    return pl.BlockSpec(memory_space=pltpu.VMEM)


def smem():
    return pl.BlockSpec(memory_space=pltpu.SMEM)


def params():
    return pltpu.CompilerParams(vmem_limit_bytes=16 * MIB)


def norm_column(points, scale):
    wide = points.astype(F32)
    return jnp.sum(wide * wide, axis=1, keepdims=True) * scale


def norm_row(points, scale):
    column = norm_column(points, scale)
    return jnp.transpose(jnp.broadcast_to(column, (column.shape[0], 128)))[0:1, :]


def listed(meta, row, first, count, value):
    hit = jnp.bool_(False)
    for slot in range(count):
        hit = hit | ((meta[row, first + slot] == value) & (slot < meta[row, first + count]))
    return hit


def near_hit(meta, row, leaf):
    return listed(meta, row, 0, NEAR, leaf)


def far_hit(meta, row, node):
    return listed(meta, row, FAR_LIST, FAR, node)


def half_scale(dim):
    return 0.5 * math.log2(math.e) / dim


def kernel_sum(xpts, xsq, ypts, ysq, wts):
    dim = xpts.shape[1]
    scores = lax.dot_general(
        xpts, ypts, (((1,), (1,)), ((), ())), preferred_element_type=F32
    )
    kern = jnp.exp2(scores * (2.0 * half_scale(dim)) - xsq - ysq)
    return jnp.dot(kern.astype(BF16), wts, preferred_element_type=F32)


def call(body, kinds, scalars, arrays):
    return pl.pallas_call(
        body,
        out_shape=kinds,
        in_specs=[smem()] * len(scalars)
        + [vmem()] * len(arrays),
        out_specs=jax.tree.map(lambda _: vmem(), kinds),
        compiler_params=params(),
        cost_estimate=pl.CostEstimate(flops=1000, bytes_accessed=1000, transcendentals=0),
    )(*scalars, *arrays)


def project_body(wts, proj, keep, *gives):
    leaf = lax.axis_index("pts")
    groups, count, wcols = keep.shape
    whole = jnp.dot(proj[...], wts[...], preferred_element_type=F32)
    whole = whole.reshape(groups, QUAD, count, wcols)
    for turn in range(QUAD):
        block = whole[:, QUAD - 1]
        for place in range(QUAD - 1):
            block = jnp.where((leaf ^ turn) % QUAD == place, whole[:, place], block)
        if turn == 0:
            keep[...] = block
        else:
            gives[turn - 1][...] = block.astype(BF16)


def project(group, wts, proj):
    shape = (group // QUAD, proj.shape[0] // group, wts.shape[1])
    kinds = (jax.ShapeDtypeStruct(shape, F32),) + (jax.ShapeDtypeStruct(shape, BF16),) * (QUAD - 1)
    return call(project_body, kinds, (), (wts, proj))


def pack_body(idx, pts, keep, *refs):
    *got, packed = refs
    rows, dim = pts.shape
    place = lax.broadcasted_iota(jnp.int32, (rows, idx.shape[1]), 0)
    pick = (place == idx[...]).astype(F32).astype(BF16)
    packed[:, :dim] = lax.dot_general(
        pick, pts[...], (((0,), (0,)), ((), ())), preferred_element_type=F32
    ).astype(BF16)
    total = keep[0]
    for part in got:
        total = total + part[0].astype(F32)
    packed[:, dim:] = total.astype(BF16)


def pack(idx, pts, keep, got):
    shape = (idx.shape[1], pts.shape[1] + keep.shape[2])
    return call(pack_body, jax.ShapeDtypeStruct(shape, BF16), (), (idx, pts, keep, *got))


def quad_body(group, places, targets, cuts, own, meta, *refs):
    packed, refs = refs[: len(places)], refs[len(places) :]
    many = len(targets)
    xpts = []
    for size in cuts:
        xpts.append(refs[0][...] if size == 1 else jnp.concatenate([ref[...] for ref in refs[:size]], axis=0))
        refs = refs[size:]
    if own:
        mine, mine_w, *outs = refs
    else:
        start, outs = refs[:many], refs[many:]
    dim = xpts[0].shape[1]
    scale = half_scale(dim)
    quads = lax.axis_size("pts") // QUAD
    leaf = meta[0, LEAF]
    quad = leaf // QUAD
    count = packed[0].shape[0]
    nodes = []
    for turn, flip in places:
        deep = (quad // 2 - turn + quads // 2) % (quads // 2)
        nodes.append((deep * 2 + (quad + flip) % 2) * QUAD // group)
    everything = jnp.concatenate([ref[...] for ref in packed], axis=0)
    ypts, wts = everything[:, :dim], everything[:, dim:]
    ysq = norm_row(ypts, scale)
    if own:
        own_sq = norm_row(mine[...], scale)
    for place, target in enumerate(targets):
        hits = [far_hit(meta, target, node) for node in nodes]
        some = functools.reduce(jnp.logical_or, hits)
        away = [jnp.full((1, count), jnp.where(hit, 0.0, 1e30), F32) for hit in hits]
        far_sq = ysq + jnp.concatenate(away, axis=1)
        xsq = norm_column(xpts[place], scale)

        def far(place=place, xsq=xsq, far_sq=far_sq):
            return kernel_sum(xpts[place], xsq, ypts, far_sq, wts)

        out = outs[place]
        if own:
            def near(place=place, xsq=xsq):
                return kernel_sum(xpts[place], xsq, mine[...], own_sq, mine_w[...])

            if target == 0:
                out[...] = near()
            else:
                hit = near_hit(meta, target, leaf)

                @pl.when(hit)
                def _(out=out, near=near):
                    out[...] = near()

                @pl.when(jnp.logical_not(hit))
                def _(out=out):
                    out[...] = jnp.zeros_like(out)

            @pl.when(some)
            def _(out=out, far=far):
                out[...] += far()
        else:
            @pl.when(some)
            def _(out=out, far=far, place=place):
                out[...] = (start[place][...] + far()).astype(out.dtype)

            @pl.when(jnp.logical_not(some))
            def _(out=out, place=place):
                out[...] = start[place][...].astype(out.dtype)


def quad_terms(group, places, targets, meta, packed, xpts, mine, start, kinds):
    rows = sum(part.shape[0] for part in xpts[0])
    wcols = packed[0].shape[1] - xpts[0][0].shape[1]
    cuts = tuple(len(parts) for parts in xpts)
    body = functools.partial(quad_body, group, tuple(places), targets, cuts, bool(mine))
    shapes = tuple(jax.ShapeDtypeStruct((rows, wcols), kind) for kind in kinds)
    return call(body, shapes, (meta,), (*packed, *sum(xpts, ()), *mine, *start))


def sum_body(one, two, out):
    out[...] = (one[...] + two[...].astype(F32)).astype(BF16)


def sum_terms(one, two):
    return call(sum_body, jax.ShapeDtypeStruct(one.shape, BF16), (), (one, two))


def cross_body(row, more, meta, xpts, start, ypts, wts, *refs):
    extras, outs = refs[:more], refs[more:]
    leaf = meta[0, LEAF]
    scale = half_scale(xpts.shape[1])
    hit = near_hit(meta, row, leaf + 4 * (leaf // 2 % 2) - 2)

    def put(value):
        for extra in extras:
            value = value + extra[...].astype(F32)
        first = 0
        for out in outs:
            out[...] = value[first : first + out.shape[0]].astype(out.dtype)
            first += out.shape[0]

    @pl.when(hit)
    def _():
        xsq, ysq = norm_column(xpts[...], scale), norm_row(ypts[...], scale)
        put(start[...] + kernel_sum(xpts[...], xsq, ypts[...], ysq, wts[...]))

    @pl.when(jnp.logical_not(hit))
    def _():
        put(start[...])


def cross_terms(row, meta, xpts, start, ypts, wts, kind, cuts, extras=()):
    rows, wcols = start.shape
    shapes = (jax.ShapeDtypeStruct((rows // cuts, wcols), kind),) * cuts
    body = functools.partial(cross_body, row, len(extras))
    return call(body, shapes, (meta,), (xpts, start, ypts, wts, *extras))


def finish_body(acc, upper, lower, out, here, sems):
    rows = acc.shape[0] // PIECES
    copies = []
    for piece in range(PIECES):
        part = pl.ds(piece * rows, rows)
        half, first = divmod(piece * rows, upper.shape[0])
        other = (upper, lower)[half][first : first + rows]
        here[part, :] = acc[part, :] + other.astype(F32)
        copy = pltpu.make_async_copy(here.at[part], out.at[part], sems.at[piece])
        copy.start()
        copies.append(copy)
    for copy in copies:
        copy.wait()


def finish(acc, upper, lower):
    return pl.pallas_call(
        finish_body,
        out_shape=jax.ShapeDtypeStruct(acc.shape, F32),
        in_specs=[vmem()] * 3,
        out_specs=pl.BlockSpec(memory_space=pl.ANY),
        scratch_shapes=[pltpu.VMEM(acc.shape, F32), pltpu.SemaphoreType.DMA((PIECES,))],
        compiler_params=params(),
        cost_estimate=pl.CostEstimate(flops=1000, bytes_accessed=1000, transcendentals=0),
    )(acc, upper, lower)


def shards(points, weights, node_proj, skel_idx, near_list, near_count, far_list, far_count):
    leaves = lax.axis_size("pts")
    me = lax.axis_index("pts")
    group = leaves // NODES
    quads = leaves // QUAD
    depth = quads // 2

    def move(value, where):
        pairs = [(source, where(source)) for source in range(leaves)]
        return lax.ppermute(value, "pts", [(a, b) for a, b in pairs if b is not None])

    def bit(level):
        return lambda source: source ^ (1 << level)

    def deeper(turn):
        def where(source):
            quad, place = divmod(source, QUAD)
            deep, side = divmod(quad, 2)
            return ((deep + turn) % depth * 2 + side) * QUAD + place

        return where

    def after(values):
        return lax.optimization_barrier(values)

    def along(way):
        def where(source):
            target = source - way * QUAD if source // 2 % 2 else source + way * QUAD
            return target if 0 <= target < leaves else None

        return where

    core, side, row = bit(0), bit(1), bit(2)

    keep, *give = project(group, weights, node_proj)
    got = [move(block, lambda source, turn=turn: source ^ turn) for turn, block in enumerate(give, 1)]
    level = 2
    while keep.shape[0] > 1:
        for part in got:
            keep = keep + part.astype(F32)
        count = keep.shape[0]
        keep = keep.reshape(count // 2, 2, *keep.shape[1:])
        upper = (me >> level) % 2 == 1
        give = jnp.where(upper, keep[:, 0], keep[:, 1]).astype(BF16)
        keep = jnp.where(upper, keep[:, 1], keep[:, 0])
        got = [move(give, bit(level))]
        level += 1
    cross_w = move(weights, along(-1))
    cut = weights.shape[0] * 11 // 256 * 16
    cross_w = [move(part, core) for part in jnp.split(cross_w, [cut])]
    got, pts_later = after((got, points))
    packed = pack(skel_idx, points, keep, got)

    up, down = deeper(1), deeper(depth - 1)
    top = depth // 2
    gathered = {(0, 0): packed}
    pts_side = move(pts_later, side)
    pts_core = move(pts_later, core)
    gathered[1, 0] = move(packed, up)
    gathered[0, 1] = move(packed, row)
    gathered, packed, cross_w = after((gathered, packed, cross_w))
    if depth > 2:
        gathered[depth - 1, 0] = move(packed, down)
    gathered[1, 1] = move(gathered[1, 0], row)
    meta = [near_list[0], near_count, far_list[0], far_count, me[None]]
    meta = jnp.concatenate(meta + [jnp.zeros((META - LEAF - 1,), jnp.int32)])[None]
    for hop in (core, side):
        meta = jnp.concatenate([meta, move(meta, hop)], axis=0)
    gathered, pts_side, meta = after((gathered, pts_side, meta))
    cross_w = move(move(jnp.concatenate(cross_w, axis=0), side), core)
    cross_p = move(pts_side, along(1))
    pts_both = (move(pts_side, core),)
    first_places = sorted(set(gathered) - {(1, 1)})
    if depth > 2:
        gathered[depth - 1, 1] = move(gathered[depth - 1, 0], row)
    for flip in range(2):
        for turn in range(2, top + 1):
            gathered[turn, flip] = move(gathered[turn - 1, flip], up)
        for turn in range(depth - 2, top, -1):
            gathered[turn, flip] = move(gathered[turn + 1, flip], down)

    mine = (points, weights)
    near_x = ((points,), (pts_core,))
    side_x = ((pts_side,), pts_both)
    some = [gathered[place] for place in first_places]
    acc0, acc1 = quad_terms(group, first_places, (0, 1), meta, some, near_x, mine, (), (F32, F32))
    acc2, acc3 = quad_terms(group, first_places, (2, 3), meta, some, side_x, mine, (), (F32, F32))
    gathered, acc0, acc1, acc2, acc3 = after((gathered, acc0, acc1, acc2, acc3))

    last_places = sorted(set(gathered) - set(first_places))
    rest = [gathered[place] for place in last_places]
    (out3,) = quad_terms(group, last_places, (3,), meta, rest, (pts_both,), (), (acc3,), (BF16,))
    got3 = move(out3, core)
    (acc2,) = quad_terms(group, last_places, (2,), meta, rest, ((pts_side,),), (), (acc2,), (F32,))
    last = move(sum_terms(acc2, got3), side)
    acc0, acc1 = quad_terms(
        group, last_places, (0, 1), meta, rest, near_x, (), (acc0, acc1), (F32, F32)
    )
    out1 = cross_terms(1, meta, pts_core, acc1, cross_p, cross_w, BF16, 2)
    (acc0,) = cross_terms(0, meta, points, acc0, cross_p, cross_w, F32, 1, (last,))
    return finish(acc0, *[move(half, core) for half in out1])


def solution(mesh):
    in_specs = (
        P("pts", None),
        P("pts", None),
        P(None, "pts"),
        P("pts", None),
        P("pts", None),
        P("pts"),
        P("pts", None),
        P("pts"),
    )
    out_specs = P("pts", None)
    return jax.shard_map(shards, mesh=mesh, in_specs=in_specs, out_specs=out_specs, check_vma=False)
```
